768 devices in a mesh: blk: 16 (over x, z_lo), table: 48 (over y, z_hi, core).
Axes of the slice: x: 4, y: 8, z: 12 (z_hi: 3, z_lo: 4; z = z_hi * 4 + z_lo), core: 2. Of those that a mesh axis runs over, the one named last changes fastest.
Arguments:
- id_table: bfloat16 [393216, 256], P('table'), may hold values from -6 to 6
- w_first: bfloat16 [256, 4096], replicated, may hold values from -0.375 to 0.375
- w_second: bfloat16 [4096, 256], replicated, may hold values from -0.09375 to 0.09375
- owner_ids: int32 [196608, 8], P(('blk', 'table')), may hold values from 0 to 47, all different within a row; in each aligned block of 256 rows (0 to 255, 256 to 511, ...) at most 64 rows name the same one
- row_ids: int32 [196608, 8], P(('blk', 'table')), may hold values from 0 to 8191
Outputs:
- loss: float32 [196608], P(('blk', 'table'))
- item_grad: float32 [196608, 256], P(('blk', 'table'))
- query_grad: float32 [196608, 256], P(('blk', 'table'))
The draws below stay inside these ranges and needn't reach their ends.
Inputs may be any that keep to these rules, and one draw needn't show every extreme that they name: `owner_ids`: the 8 ids of one pair name 8 different shards; among the ids of one device's 256 pairs no shard is named more than 64 times, a bound that some block reaches.
All inputs are finite; a program needn't handle non-finite values.
Results may differ from the reference program's by a relative error of at most 0.0056.
Values may be sent and summed in bfloat16 or wider, within the bound.
A program may use at most 64 MiB of HBM per device.

```python
import math
import jax
import jax.numpy as jnp
import numpy as np
from jax import lax

E = 256
H = 4096
B_DEV = 256
BAGS = 8
ROWS_DEV = 8192
CAP = 64
PAIRS = 196608
ROWS = 393216
N_BLK = 16
N_TABLE = 48


def set_ends(drawn, own_key, low, top_value):
    dims = drawn.shape
    spot = [jax.random.randint(jax.random.fold_in(own_key, axis), (), 0, dims[axis]) for axis in range(len(dims))]
    drawn = drawn.at[tuple(spot)].set(low)
    longest = dims.index(max(dims))
    spot[longest] = (spot[longest] + 1) % dims[longest]
    return drawn.at[tuple(spot)].set(top_value)


def levels(stream_key, shape, cuts, low, high):
    gain, own = 1.0, jax.random.fold_in(stream_key, 6)
    for axis_at, blocks in cuts:
        draws = jnp.exp(jax.random.uniform(jax.random.fold_in(own, axis_at), (blocks,), jnp.float32, low / len(cuts), high / len(cuts)))
        gain = gain * jnp.repeat(draws, shape[axis_at] // blocks).reshape([-1 if axis == axis_at else 1 for axis in range(len(shape))])
    return gain


def routed_block(own_key, own, number, rows, amount, top, most, lean):
    order = jax.random.permutation(own_key, amount)
    packed, usual = portions_of(amount, rows * top, most, lean, True), portions_of(amount, rows * top, most, lean, False)
    places = jnp.arange(amount)

    def named(lengths, offset_by):
        used = int((lengths > 0).sum())
        fixed = max(1, used // 4)
        moved = fixed + (places - fixed + offset_by * (used - fixed)) % max(1, amount - fixed)
        return jnp.zeros((amount,), jnp.int32).at[order[jnp.where(places < fixed, places, moved)]].set(jnp.asarray(lengths, jnp.int32))

    lengths = jnp.where(number % 4 == 0, named(packed, number // 4), named(usual, number - number // 4 - 1))
    mixed = jax.random.permutation(jax.random.fold_in(own, 3), amount)
    source_of, sink = mixed[0:amount // 2 * 2:2], mixed[1:amount // 2 * 2:2]
    margin = jnp.minimum(lengths[source_of] - 1, most - lengths[sink]) // 2
    margin = jnp.where((source_of == order[0]) | (sink == order[0]) | (lengths[sink] == 0), 0, jnp.maximum(margin, 0))
    moved = jax.random.randint(jax.random.fold_in(own, 4), (amount // 2,), 0, 1 << 20) % (margin + 1)
    lengths = lengths.at[source_of].add(-moved).at[sink].add(moved)
    members = jnp.searchsorted(jnp.cumsum(lengths), jnp.arange(rows * top), side="right").astype(jnp.int32)
    table = members.reshape(top, rows).T
    table = table[jax.random.permutation(jax.random.fold_in(own, 1), rows)]
    offset_by = jax.random.randint(jax.random.fold_in(own, 2), (rows, 1), 0, top)
    return jnp.take_along_axis(table, (jnp.arange(top)[None, :] + offset_by) % top, axis=1)


def portions_of(number_of, total, bound, skew, full):
    loads = [(1 << 20) // math.isqrt(grade ** skew) + 1 for grade in range(1, number_of + 1)]
    largest = bound if full else min(bound, max(-(-total // number_of), total * loads[0] // sum(loads)))
    least = 1 if total - largest >= number_of - 1 else 0
    given, rest = [largest] + [least] * (number_of - 1), total - largest - least * (number_of - 1)
    while rest > 0:
        candidates = [i for i in range(1, number_of) if given[i] < largest] or [i for i in range(1, number_of) if given[i] < bound]
        whole, left = sum([loads[i] for i in candidates]), rest
        for i in candidates:
            addition = min(bound - given[i], max(1, left * loads[i] // whole), rest)
            given[i] = given[i] + addition
            rest = rest - addition
    return np.array(given)


def centred(stream_key, extent, width, reach, cuts=(), dtype=jnp.bfloat16):
    values = jax.random.normal(stream_key, extent, jnp.float32) * width
    if len(cuts) > 0:
        values = levels(stream_key, extent, cuts, -0.22, 0.18) * values
    return jnp.clip(values, min=-reach, max=reach).astype(dtype)


def setup_inputs(seed: int = 0) -> dict:
    key_of = jax.random.split(jax.random.key(seed), 6)
    id_table = centred(key_of[0], (ROWS, E), 1.0, 6.0, ((0, 48),))
    w_first = centred(key_of[1], (E, H), E ** -0.5, 0.375)
    w_second = centred(key_of[2], (H, E), H ** -0.5, 0.09375)
    owner_ids_keys = jax.random.split(jax.random.fold_in(key_of[3], 1), PAIRS // B_DEV)
    owner_ids_turns = jax.random.permutation(jax.random.fold_in(key_of[3], 3), PAIRS // B_DEV)
    owner_ids = jax.vmap(lambda own, number: routed_block(jax.random.fold_in(key_of[3], 2), own, number, B_DEV, N_TABLE, BAGS, CAP, 2))(owner_ids_keys, owner_ids_turns).reshape((PAIRS, BAGS))
    row_ids = set_ends(jax.random.randint(key_of[4], (PAIRS, BAGS), 0, ROWS_DEV), jax.random.fold_in(key_of[4], 1), 0, ROWS_DEV - 1).astype(jnp.int32)
    return {"id_table": id_table, "w_first": w_first, "w_second": w_second, "owner_ids": owner_ids, "row_ids": row_ids}


EPS = 1e-06
INV_TEMP = 20.0

def silu_slope(pre):
    sigma = jax.nn.sigmoid(pre)
    return sigma * (1.0 + pre * (1.0 - sigma))

def unit_rows(vectors):
    scale = lax.rsqrt(lax.optimization_barrier(jnp.sum(vectors * vectors, axis=-1, keepdims=True)) + EPS)
    return (vectors * scale, scale)

def unit_backward(grad, unit, scale):
    return scale * (grad - unit * lax.optimization_barrier(jnp.sum(unit * grad, axis=-1, keepdims=True)))

def row_dot(left, right):
    return lax.dot_general(left, right, (((1,), (1,)), ((), ())), preferred_element_type=jnp.float32)

def col_dot(left, right):
    return lax.dot_general(left, right, (((0,), (0,)), ((), ())), preferred_element_type=jnp.float32)

def reference(id_table, w_first, w_second, owner_ids, row_ids):
    half = BAGS // 2

    def regroup(values):
        shaped = values.reshape((N_BLK, N_TABLE, B_DEV) + values.shape[1:])
        shaped = jnp.swapaxes(shaped, 0, 1)
        return shaped.reshape((N_TABLE, N_BLK * B_DEV) + values.shape[1:])

    def ungroup(values):
        shaped = values.reshape((N_TABLE, N_BLK, B_DEV) + values.shape[2:])
        shaped = jnp.swapaxes(shaped, 0, 1)
        return shaped.reshape((PAIRS,) + values.shape[2:])

    def group(pieces):
        owners, rows = pieces
        flat = (owners * ROWS_DEV + rows).astype(jnp.int32)
        embedded = jnp.take(id_table, flat, axis=0).astype(jnp.float32)
        query_in = lax.optimization_barrier(jnp.sum(embedded[:, :half], axis=1)).astype(jnp.bfloat16)
        item_in = lax.optimization_barrier(jnp.sum(embedded[:, half:], axis=1))
        hidden_pre = jnp.dot(query_in, w_first, preferred_element_type=jnp.float32)
        hidden = jax.nn.silu(hidden_pre).astype(jnp.bfloat16)
        query_out = jnp.dot(hidden, w_second, preferred_element_type=jnp.float32)
        query_unit, query_scale = unit_rows(query_out)
        item_unit, item_scale = unit_rows(item_in)
        query_bf = query_unit.astype(jnp.bfloat16)
        item_bf = item_unit.astype(jnp.bfloat16)
        scores = INV_TEMP * row_dot(query_bf, item_bf)
        log_total = jnp.log(lax.optimization_barrier(jnp.sum(jnp.exp(scores), axis=1)))
        own = INV_TEMP * lax.optimization_barrier(jnp.sum(query_bf.astype(jnp.float32) * item_bf.astype(jnp.float32), axis=1))
        loss = log_total - own
        probs = jnp.exp(scores - log_total[:, None]).astype(jnp.bfloat16)
        query_sum = jnp.dot(probs, item_bf, preferred_element_type=jnp.float32)
        item_sum = col_dot(probs, query_bf)
        query_unit_grad = INV_TEMP * (query_sum - item_bf.astype(jnp.float32))
        item_unit_grad = INV_TEMP * (item_sum - query_bf.astype(jnp.float32))
        item_grad = unit_backward(item_unit_grad, item_unit, item_scale)
        out_grad = unit_backward(query_unit_grad, query_unit, query_scale).astype(jnp.bfloat16)
        hidden_grad = (row_dot(out_grad, w_second) * silu_slope(hidden_pre)).astype(jnp.bfloat16)
        query_grad = row_dot(hidden_grad, w_first)
        return (loss, item_grad, query_grad)
    loss, item_grad, query_grad = lax.map(group, (regroup(owner_ids), regroup(row_ids)))
    return (ungroup(loss), ungroup(item_grad), ungroup(query_grad))
```

```python
import functools
import math

import jax
import jax.numpy as jnp
from jax import lax
from jax.experimental import pallas as pl
from jax.experimental.pallas import tpu as pltpu
from jax.sharding import PartitionSpec as P

EPS = 1e-06
INV_TEMP = 20.0
MESH = pl.DeviceIdType.MESH
F32 = jnp.float32
BF16 = jnp.bfloat16


def row_dot(left, right):
    return lax.dot_general(left, right, (((1,), (1,)), ((), ())), preferred_element_type=F32)


def col_dot(left, right):
    return lax.dot_general(left, right, (((0,), (0,)), ((), ())), preferred_element_type=F32)


def dot(left, right):
    return jnp.dot(left, right, preferred_element_type=F32)


def unit_rows(vectors):
    scale = lax.rsqrt(jnp.sum(vectors * vectors, axis=-1, keepdims=True) + EPS)
    return vectors * scale, scale


def unit_backward(grad, unit, scale):
    return scale * (grad - unit * jnp.sum(unit * grad, axis=-1, keepdims=True))


def lookup_kernel(
    n, cap, owner_ref, row_ref, table_ref, query_ref, item_ref,
    table_bf, table_wide, req_all, req_out, req_in, req_smem, rows_out, rows_in, select, stage, total,
    local_sem, req_send, req_recv, rows_send, rows_recv,
):
    me = lax.axis_index("table")
    pairs, bags = owner_ref.shape
    shard_rows = table_ref.shape[0]
    step_rows = stage.shape[0]
    chunks, _, chunk = select.shape

    fetch = pltpu.make_async_copy(table_ref, table_bf, local_sem.at[0])
    fetch.start()
    barrier = pltpu.get_barrier_semaphore()

    def greet(step, _):
        peer = lax.rem(me + step, n)
        pl.semaphore_signal(barrier, inc=1, device_id={"table": peer}, device_id_type=MESH)
        return 0

    lax.fori_loop(1, n, greet, 0)

    lanes = req_all.shape[0]
    wide = 2 * cap
    shard_lane = lax.broadcasted_iota(jnp.int32, (pairs, lanes), 1)
    slot_lane = lax.broadcasted_iota(jnp.int32, (pairs, wide), 1)
    upper_half = slot_lane >= cap
    slot_of_lane = jnp.where(upper_half, slot_lane - cap, slot_lane)
    earlier = jnp.where(
        lax.broadcasted_iota(jnp.int32, (pairs, pairs), 0)
        > lax.broadcasted_iota(jnp.int32, (pairs, pairs), 1),
        1.0, 0.0,
    ).astype(BF16)
    counts = jnp.zeros((1, lanes), F32)
    wanted = jnp.zeros((lanes, wide), F32)
    places = []
    for k in range(bags):
        owner = owner_ref[:, k : k + 1]
        row = row_ref[:, k : k + 1]
        hot = jnp.where(owner == shard_lane, 1.0, 0.0)
        hot_bf = hot.astype(BF16)
        before = dot(earlier, hot_bf) + counts
        slot = jnp.sum(hot * before, axis=1, keepdims=True).astype(jnp.int32)
        counts = counts + jnp.sum(hot, axis=0, keepdims=True)
        digit = jnp.where(upper_half, row & 127, row >> 7).astype(F32)
        digit = jnp.where(slot_of_lane == slot, digit, 0.0).astype(BF16)
        wanted = wanted + col_dot(hot_bf, digit)
        places.append(owner * cap + slot)
    wanted = wanted * 128.0 + pltpu.roll(wanted, cap, 1)
    req_all[...] = wanted.astype(jnp.int32)

    def split(shard, _):
        req_out[shard] = req_all[pl.ds(shard, 1), :]
        return 0

    lax.fori_loop(0, n, split, 0)
    req_in[me] = req_out[me]
    pl.semaphore_wait(barrier, n - 1)

    def request(peer):
        return pltpu.make_async_remote_copy(
            src_ref=req_out.at[peer], dst_ref=req_in.at[me],
            send_sem=req_send.at[peer], recv_sem=req_recv.at[me],
            device_id={"table": peer}, device_id_type=MESH,
        )

    def ask(step, _):
        request(lax.rem(me + step, n)).start()
        return 0

    lax.fori_loop(1, n, ask, 0)

    fetch.wait()
    blocks = 32
    block_rows = shard_rows // blocks

    def widen(block, _):
        at = pl.ds(pl.multiple_of(block * block_rows, block_rows), block_rows)
        table_wide[at, :] = table_bf[at, :].astype(F32)
        return 0

    lax.fori_loop(0, blocks, widen, 0)

    half = bags // 2

    def choose(block, _):
        column = lax.broadcasted_iota(jnp.int32, (pairs, chunk), 1) + block * chunk
        for side in range(2):
            mask = places[side * half] == column
            for k in range(side * half + 1, (side + 1) * half):
                mask = mask | (places[k] == column)
            select[block, side * pairs : (side + 1) * pairs, :] = jnp.where(mask, 1.0, 0.0).astype(BF16)
        return 0

    lax.fori_loop(0, chunks, choose, 0)

    def asked(step, _):
        peer = lax.rem(me + step, n)
        pltpu.make_async_remote_copy(
            src_ref=req_out.at[peer], dst_ref=req_in.at[peer],
            send_sem=req_send.at[peer], recv_sem=req_recv.at[peer],
            device_id={"table": peer}, device_id_type=MESH,
        ).wait()
        return 0

    lax.fori_loop(1, n, asked, 0)
    to_smem = pltpu.make_async_copy(req_in, req_smem, local_sem.at[1])
    to_smem.start()
    to_smem.wait()

    def gather(peer, target, start):
        def some(part, _):
            for s in range(step_rows):
                index = req_smem[peer, 0, part * step_rows + s] & (shard_rows - 1)
                stage[s : s + 1, :] = table_wide[pl.ds(index, 1), :]
            at = pl.multiple_of(start + part * step_rows, step_rows)
            target[pl.ds(at, step_rows), :] = stage[...].astype(BF16)
            return 0

        lax.fori_loop(0, cap // step_rows, some, 0)

    def sending(peer, slot):
        return pltpu.make_async_remote_copy(
            src_ref=rows_out.at[pl.ds(pl.multiple_of(peer * cap, cap), cap), :],
            dst_ref=rows_in.at[pl.ds(pl.multiple_of(slot * cap, cap), cap), :],
            send_sem=rows_send.at[peer], recv_sem=rows_recv.at[slot],
            device_id={"table": peer}, device_id_type=MESH,
        )

    def serve(step, _):
        away = n // 2 - (step + 1) // 2
        offset = away + (step % 2) * (n - 2 * away)
        peer = lax.rem(me + offset, n)
        gather(peer, rows_out, peer * cap)
        sending(peer, me).start()
        return 0

    lax.fori_loop(0, n - 1, serve, 0)
    gather(me, rows_in, me * cap)

    total[...] = jnp.zeros_like(total)

    def arrived(source, _):
        @pl.when(source != me)
        def _():
            sending(source, source).wait()

        return 0

    def combine(block, _):
        each = chunk // cap
        lax.fori_loop(block * each, (block + 1) * each, arrived, 0)
        at = pl.ds(pl.multiple_of(block * chunk, chunk), chunk)
        total[...] += dot(select[block], rows_in[at, :])
        return 0

    lax.fori_loop(0, chunks, combine, 0)
    query_ref[...] = total[0:pairs, :].astype(BF16)
    item_ref[...] = total[pairs : 2 * pairs, :]


def lookup(n, id_table, owner_ids, row_ids):
    pairs, bags = owner_ids.shape
    width = id_table.shape[1]
    cap = min(pairs, 3 * pairs * bags // (2 * n))
    lanes = max(128, n)
    slots = n * cap
    chunk = min(slots, 8 * cap)
    vmem = pl.BlockSpec(memory_space=pltpu.VMEM)
    return pl.pallas_call(
        functools.partial(lookup_kernel, n, cap),
        out_shape=(
            jax.ShapeDtypeStruct((pairs, width), BF16),
            jax.ShapeDtypeStruct((pairs, width), F32),
        ),
        in_specs=[vmem, vmem, pl.BlockSpec(memory_space=pl.ANY)],
        out_specs=(vmem, vmem),
        scratch_shapes=[
            pltpu.VMEM(id_table.shape, BF16),
            pltpu.VMEM(id_table.shape, F32),
            pltpu.VMEM((lanes, 2 * cap), jnp.int32),
            pltpu.VMEM((n, 1, 2 * cap), jnp.int32),
            pltpu.VMEM((n, 1, 2 * cap), jnp.int32),
            pltpu.SMEM((n, 1, 2 * cap), jnp.int32),
            pltpu.VMEM((slots, width), BF16),
            pltpu.VMEM((slots, width), BF16),
            pltpu.VMEM((slots // chunk, 2 * pairs, chunk), BF16),
            pltpu.VMEM((16, width), F32),
            pltpu.VMEM((2 * pairs, width), F32),
            pltpu.SemaphoreType.DMA((2,)),
            pltpu.SemaphoreType.DMA((n,)),
            pltpu.SemaphoreType.DMA((n,)),
            pltpu.SemaphoreType.DMA((n,)),
            pltpu.SemaphoreType.DMA((n,)),
        ],
        compiler_params=pltpu.CompilerParams(
            collective_id=0, has_side_effects=True, vmem_limit_bytes=48 * 2**20
        ),
        name="lookup",
    )(owner_ids, row_ids, id_table)


def train_kernel(
    nx, nz, query_ref, item_ref, first_hbm, second_hbm, loss_ref, item_grad_ref, query_grad_ref,
    first, second, slope, items, queries, exps, total_out, total_in,
    query_out, query_in, item_sum, item_out, item_in, acc,
    local_sem, send_sem, recv_sem,
):
    blk = lax.axis_index("blk")
    x, z = blk // nz, blk % nz
    pairs, width = query_ref.shape
    steps, chunk = slope.shape[0], slope.shape[2]

    load_first = pltpu.make_async_copy(first_hbm, first, local_sem.at[0])
    load_second = pltpu.make_async_copy(second_hbm, second, local_sem.at[1])
    load_first.start()
    load_second.start()

    def along_x(step):
        there = lax.rem(x + step, nx)
        return there, there * nz + z

    def along_z(step):
        there = lax.rem(z + step, nz)
        return there, x * nz + there

    barrier = pltpu.get_barrier_semaphore()
    for axis, count in ((along_x, nx), (along_z, nz)):
        for step in range(1, count):
            pl.semaphore_signal(
                barrier, inc=1, device_id={"blk": axis(step)[1]}, device_id_type=MESH
            )

    item_unit, item_scale = unit_rows(item_ref[...])
    items[z] = item_unit.astype(BF16)
    pl.semaphore_wait(barrier, nx + nz - 2)

    def copy(phase, source, target, landing, step, axis):
        there, device = axis(step)
        return pltpu.make_async_remote_copy(
            src_ref=source, dst_ref=target,
            send_sem=send_sem.at[phase, there], recv_sem=recv_sem.at[phase, landing],
            device_id={"blk": device}, device_id_type=MESH,
        )

    def item_copy(step, slot):
        return copy(0, items.at[z], items.at[slot], slot, step, along_z)

    def query_copy(step, slot):
        return copy(1, queries.at[x], queries.at[slot], slot, step, along_x)

    def total_copy(step, slot):
        return copy(2, total_out, total_in.at[slot], slot, step, along_x)

    def query_sum_copy(step, slot):
        there = along_x(step)[0]
        return copy(3, query_out.at[there], query_in.at[slot], slot, step, along_x)

    def item_sum_copy(step, slot):
        there = along_z(step)[0]
        return copy(4, item_out.at[there], item_in.at[slot], slot, step, along_z)

    for step in range(1, nz):
        item_copy(step, z).start()

    acc[...] = jnp.zeros_like(acc)
    load_first.wait()
    load_second.wait()

    def forward(part, _):
        at = pl.ds(pl.multiple_of(part * chunk, chunk), chunk)
        pre = dot(query_ref[...], first[:, at])
        sigma = 0.5 + 0.5 * jnp.tanh(0.5 * pre)
        slope[part] = sigma * (1.0 + pre * (1.0 - sigma))
        acc[...] += dot((pre * sigma).astype(BF16), second[at, :])
        return 0

    lax.fori_loop(0, steps, forward, 0)
    query_unit, query_scale = unit_rows(acc[...])
    queries[x] = query_unit.astype(BF16)
    for step in range(1, nx):
        query_copy(step, x).start()

    diagonal = lax.broadcasted_iota(jnp.int32, (pairs, pairs), 0) == lax.broadcasted_iota(
        jnp.int32, (pairs, pairs), 1
    )

    own = None
    for step in range(nx):
        xi = along_x(step)[0]
        if step > 0:
            query_copy(step, xi).wait_recv()
        part = jnp.zeros((1, pairs), F32)
        for turn in range(nz):
            zi = along_z(turn)[0]
            if step == 0 and turn > 0:
                item_copy(turn, zi).wait_recv()
            scores = INV_TEMP * row_dot(items[zi], queries[xi])
            if step == 0 and turn == 0:
                own = jnp.sum(jnp.where(diagonal, scores, 0.0), axis=0, keepdims=True)
            value = jnp.exp(scores)
            exps[step, zi] = value
            part = part + jnp.sum(value, axis=0, keepdims=True)
        total_out[xi] = part
    total_in[x] = total_out[...]
    for step in range(1, nx):
        total_copy(step, x).start()
    for step in range(1, nx):
        total_copy(step, along_x(step)[0]).wait_recv()

    all_items = items[...].reshape(nz * pairs, width)
    query_sum = None
    for turn in range(nx):
        step = (turn + 1) % nx
        xi = along_x(step)[0]
        total = jnp.zeros((1, pairs), F32)
        for source in range(nx):
            total = total + total_in[source, xi]
        if step == 0:
            loss_ref[...] = jnp.log(total) - own
        prob = (exps[step].reshape(nz * pairs, pairs) * (1.0 / total)).astype(BF16)
        part = col_dot(prob, all_items)
        if step == 0:
            query_sum = part
        else:
            query_out[xi] = part.astype(BF16)
            query_sum_copy(step, x).start()
        added = dot(prob, queries[xi]).reshape(nz, pairs, width)
        item_sum[...] = added if turn == 0 else item_sum[...] + added
    for step in range(1, nz):
        zi = along_z(step)[0]
        item_out[zi] = item_sum[zi].astype(BF16)
        item_sum_copy(step, z).start()

    for step in range(1, nx):
        xi = along_x(step)[0]
        query_sum_copy(step, xi).wait_recv()
        query_sum = query_sum + query_in[xi].astype(F32)
    query_unit_grad = INV_TEMP * (query_sum - items[z].astype(F32))
    query_unit = acc[...] * query_scale
    out_grad = unit_backward(query_unit_grad, query_unit, query_scale).astype(BF16)
    acc[...] = jnp.zeros_like(acc)

    def backward(part, _):
        at = pl.ds(pl.multiple_of(part * chunk, chunk), chunk)
        hidden_grad = (row_dot(out_grad, second[at, :]) * slope[part]).astype(BF16)
        acc[...] += row_dot(hidden_grad, first[:, at])
        return 0

    lax.fori_loop(0, steps, backward, 0)
    query_grad_ref[...] = acc[...]

    total_items = item_sum[z]
    for step in range(1, nz):
        zi = along_z(step)[0]
        item_sum_copy(step, zi).wait_recv()
        total_items = total_items + item_in[zi].astype(F32)
    item_unit_grad = INV_TEMP * (total_items - queries[x].astype(F32))
    item_unit, item_scale = unit_rows(item_ref[...])
    item_grad_ref[...] = unit_backward(item_unit_grad, item_unit, item_scale)

    for step in range(1, nz):
        item_copy(step, z).wait_send()
        item_sum_copy(step, z).wait_send()
    for step in range(1, nx):
        query_copy(step, x).wait_send()
        total_copy(step, x).wait_send()
        query_sum_copy(step, x).wait_send()


def train(nx, nz, query_in, item_in, w_first, w_second):
    pairs, width = query_in.shape
    hidden = w_first.shape[1]
    chunk = min(hidden, 512)
    vmem = pl.BlockSpec(memory_space=pltpu.VMEM)
    hbm = pl.BlockSpec(memory_space=pl.ANY)
    most = max(nx, nz)
    return pl.pallas_call(
        functools.partial(train_kernel, nx, nz),
        out_shape=(
            jax.ShapeDtypeStruct((1, pairs), F32),
            jax.ShapeDtypeStruct((pairs, width), F32),
            jax.ShapeDtypeStruct((pairs, width), F32),
        ),
        in_specs=[vmem, vmem, hbm, hbm],
        out_specs=(vmem, vmem, vmem),
        scratch_shapes=[
            pltpu.VMEM(w_first.shape, BF16),
            pltpu.VMEM(w_second.shape, BF16),
            pltpu.VMEM((hidden // chunk, pairs, chunk), F32),
            pltpu.VMEM((nz, pairs, width), BF16),
            pltpu.VMEM((nx, pairs, width), BF16),
            pltpu.VMEM((nx, nz, pairs, pairs), F32),
            pltpu.VMEM((nx, 1, pairs), F32),
            pltpu.VMEM((nx, nx, 1, pairs), F32),
            pltpu.VMEM((nx, pairs, width), BF16),
            pltpu.VMEM((nx, pairs, width), BF16),
            pltpu.VMEM((nz, pairs, width), F32),
            pltpu.VMEM((nz, pairs, width), BF16),
            pltpu.VMEM((nz, pairs, width), BF16),
            pltpu.VMEM((pairs, width), F32),
            pltpu.SemaphoreType.DMA((2,)),
            pltpu.SemaphoreType.DMA((5, most)),
            pltpu.SemaphoreType.DMA((5, most)),
        ],
        compiler_params=pltpu.CompilerParams(
            collective_id=1, has_side_effects=True, vmem_limit_bytes=48 * 2**20
        ),
        name="train",
    )(query_in, item_in, w_first, w_second)


def local(nx, nz, n, id_table, w_first, w_second, owner_ids, row_ids):
    query_in, item_in = lookup(n, id_table, owner_ids, row_ids)
    loss, item_grad, query_grad = train(nx, nz, query_in, item_in, w_first, w_second)
    return loss.reshape(-1), item_grad, query_grad


def solution(mesh):
    blocks, shards = mesh.shape["blk"], mesh.shape["table"]
    nx = math.isqrt(blocks)
    nz = blocks // nx
    placed = (P("table", None), P(), P(), P(("blk", "table"), None), P(("blk", "table"), None))
    return jax.shard_map(
        functools.partial(local, nx, nz, shards),
        mesh=mesh,
        in_specs=placed,
        out_specs=(P(("blk", "table")), P(("blk", "table"), None), P(("blk", "table"), None)),
        check_vma=False,
    )
```

```python
import functools
import math

import jax
import jax.numpy as jnp
from jax import lax
from jax.experimental import pallas as pl
from jax.experimental.pallas import tpu as pltpu
from jax.sharding import PartitionSpec as P

EPS = 1e-06
INV_TEMP = 20.0
MESH = pl.DeviceIdType.MESH
F32 = jnp.float32
BF16 = jnp.bfloat16


def row_dot(left, right):
    return lax.dot_general(left, right, (((1,), (1,)), ((), ())), preferred_element_type=F32)


def col_dot(left, right):
    return lax.dot_general(left, right, (((0,), (0,)), ((), ())), preferred_element_type=F32)


def dot(left, right):
    return jnp.dot(left, right, preferred_element_type=F32)


def unit_rows(vectors):
    scale = lax.rsqrt(jnp.sum(vectors * vectors, axis=-1, keepdims=True) + EPS)
    return vectors * scale, scale


def unit_backward(grad, unit, scale):
    return scale * (grad - unit * jnp.sum(unit * grad, axis=-1, keepdims=True))


def lookup(grid, meet, owner_ref, row_ref, table_ref, query_ref, item_ref, refs):
    ny, planes, cores = grid
    (table_bf, table_wide, ids, code_rows, codes, req_out, req_in, req_smem, rows_out, rows_in, select,
     stage, part_out, part_in, local_sem, ids_send, ids_recv, req_send, req_recv, rows_send, rows_recv,
     part_send, part_recv) = refs
    bags, pairs = owner_ref.shape
    shard_rows, width = table_ref.shape
    cap, half_width = rows_in.shape[3:]
    chunks, chunk = select.shape[1], select.shape[3]
    step_rows = stage.shape[0]
    half = bags // 2
    m = ny * cores
    t = lax.axis_index("table")
    plane = (t // cores) % planes
    q = t // (planes * cores) * cores + t % cores

    def shard(place, where):
        return place // cores * (planes * cores) + where * cores + place % cores

    def column(r):
        return {"table": shard(q, lax.rem(plane + r, planes))}

    def across(place):
        return {"table": shard(place, plane)}

    def around(step):
        away = m // 2 - (step + 1) // 2
        return lax.rem(q + away + (step % 2) * (m - 2 * away), m)

    fetch = pltpu.make_async_copy(table_ref, table_bf, local_sem.at[0])
    fetch.start()
    barrier = pltpu.get_barrier_semaphore()

    def greet(step, _):
        pl.semaphore_signal(barrier, inc=1, device_id=across(around(step)), device_id_type=MESH)
        return 0

    lax.fori_loop(0, m - 1, greet, 0)
    for r in range(1, planes):
        pl.semaphore_signal(barrier, inc=1, device_id=column(r), device_id_type=MESH)
    others = meet(barrier)
    ids[0] = owner_ref[...] * shard_rows + row_ref[...]
    code_rows[...] = jnp.zeros_like(code_rows)
    pl.semaphore_wait(barrier, m - 1 + planes - 1 + others)

    def ids_copy(r, slot):
        return pltpu.make_async_remote_copy(
            src_ref=ids.at[0], dst_ref=ids.at[slot], send_sem=ids_send.at[r], recv_sem=ids_recv.at[slot],
            device_id=column(r), device_id_type=MESH,
        )

    for r in range(1, planes):
        ids_copy(r, planes - r).start()

    place_iota = lax.broadcasted_iota(jnp.int32, (m, pairs), 0)
    plane_shards = place_iota + place_iota // cores * (planes * cores - cores) + plane * cores
    first_slot = (place_iota * cap).astype(F32)
    digit_iota = lax.broadcasted_iota(jnp.int32, (2 * cap, pairs), 0)
    low_digit = digit_iota >= cap
    digit_slot = jnp.where(low_digit, digit_iota - cap, digit_iota).astype(F32)
    earlier = jnp.where(
        lax.broadcasted_iota(jnp.int32, (pairs, pairs), 0)
        < lax.broadcasted_iota(jnp.int32, (pairs, pairs), 1),
        1.0, 0.0,
    ).astype(BF16)
    bits = shard_rows.bit_length() - 1

    def route(r):
        packed = ids[r]
        owner, row = packed >> bits, packed & (shard_rows - 1)
        hots = [jnp.where(owner[k : k + 1, :] == plane_shards, 1.0, 0.0) for k in range(bags)]
        before = dot(jnp.concatenate(hots, axis=0).astype(BF16), earlier)
        count = jnp.zeros((m, 1), F32)
        digits = []
        for k in range(bags):
            hot = hots[k]
            held = before[k * m : (k + 1) * m, :] + count
            inside = jnp.sum(hot, axis=0, keepdims=True)
            slot = jnp.sum(hot * held, axis=0, keepdims=True)
            code = slot + jnp.sum(hot * first_slot, axis=0, keepdims=True)
            code_rows[k : k + 1, :] = jnp.where(inside > 0.0, code, -1.0)
            digit = jnp.where(low_digit, row[k : k + 1, :] & 127, row[k : k + 1, :] >> 7).astype(F32)
            digits.append(jnp.where(digit_slot == slot, digit, 0.0).astype(BF16))
            count = count + jnp.sum(hot, axis=1, keepdims=True)
        hot_all = jnp.concatenate([hot.astype(BF16) for hot in hots], axis=1)
        wanted = row_dot(hot_all, jnp.concatenate(digits, axis=1))
        wanted = (wanted * 128.0 + pltpu.roll(wanted, cap, 1)).astype(jnp.int32)
        for place in range(m):
            req_out[place, r : r + 1, :] = wanted[place : place + 1, :]
        codes[r] = jnp.transpose(code_rows[...]).astype(jnp.int32)

    route(0)
    fetch.wait()
    blocks = 32
    block_rows = shard_rows // blocks

    def widen(block, _):
        at = pl.ds(pl.multiple_of(block * block_rows, block_rows), block_rows)
        table_wide[at, :] = table_bf[at, :].astype(F32)
        return 0

    lax.fori_loop(0, blocks, widen, 0)
    for r in range(1, planes):
        ids_copy(r, r).wait()
        route(r)

    def request(place, slot):
        return pltpu.make_async_remote_copy(
            src_ref=req_out.at[place], dst_ref=req_in.at[slot],
            send_sem=req_send.at[place], recv_sem=req_recv.at[slot],
            device_id=across(place), device_id_type=MESH,
        )

    def ask(step, _):
        request(around(step), q).start()
        return 0

    lax.fori_loop(0, m - 1, ask, 0)
    req_in[q] = req_out[q]

    def choose(r):
        def some(block, _):
            place = lax.broadcasted_iota(jnp.int32, (pairs, chunk), 1) + block * chunk
            for side in range(2):
                mask = codes[r, :, side * half : side * half + 1] == place
                for k in range(side * half + 1, (side + 1) * half):
                    mask = mask | (codes[r, :, k : k + 1] == place)
                select[r, block, side * pairs : (side + 1) * pairs, :] = jnp.where(mask, 1.0, 0.0).astype(BF16)
            return 0

        lax.fori_loop(0, chunks, some, 0)

    for r in range(1, planes):
        choose(r)

    def asked(step, _):
        place = around(step)
        request(place, place).wait()
        return 0

    lax.fori_loop(0, m - 1, asked, 0)
    to_smem = pltpu.make_async_copy(req_in, req_smem, local_sem.at[1])
    to_smem.start()
    to_smem.wait()

    def gather(place, r, left, right):
        def some(part, _):
            for s in range(step_rows):
                index = req_smem[place, r, part * step_rows + s] & (shard_rows - 1)
                stage[s : s + 1, :] = table_wide[pl.ds(index, 1), :]
            at = pl.ds(pl.multiple_of(part * step_rows, step_rows), step_rows)
            rows = stage[...].astype(BF16)
            left[at, :] = rows[:, :half_width]
            right[at, :] = rows[:, half_width:]
            return 0

        lax.fori_loop(0, cap // step_rows, some, 0)

    foreign = pl.ds(1, planes - 1)

    def foreign_copy(side, place, slot):
        return pltpu.make_async_remote_copy(
            src_ref=rows_out.at[side, place, foreign], dst_ref=rows_in.at[side, foreign, slot],
            send_sem=rows_send.at[side, place], recv_sem=rows_recv.at[side, slot],
            device_id=across(place), device_id_type=MESH,
        )

    def near_copy(place, slot):
        return pltpu.make_async_remote_copy(
            src_ref=rows_out.at[:, place, 0], dst_ref=rows_in.at[:, 0, slot],
            send_sem=rows_send.at[2, place], recv_sem=rows_recv.at[2, slot],
            device_id=across(place), device_id_type=MESH,
        )

    def serve_foreign(step, _):
        place = around(step)
        for r in range(1, planes):
            gather(place, r, rows_out.at[0, place, r], rows_out.at[1, place, r])
        foreign_copy(0, place, q).start()
        return 0

    def serve_second(step, _):
        foreign_copy(1, around(step), q).start()
        return 0

    def serve_near(step, _):
        place = around(step)
        gather(place, 0, rows_out.at[0, place, 0], rows_out.at[1, place, 0])
        near_copy(place, q).start()
        return 0

    lax.fori_loop(0, m - 1, serve_foreign, 0)
    lax.fori_loop(0, m - 1, serve_second, 0)
    lax.fori_loop(0, m - 1, serve_near, 0)
    for r in range(planes):
        gather(q, r, rows_in.at[0, r, q], rows_in.at[1, r, q])

    def bag_sums(side, r):
        rows = rows_in[side, r].reshape(m * cap, half_width)
        total = dot(select[r, 0], rows[:chunk])
        for block in range(1, chunks):
            total = total + dot(select[r, block], rows[block * chunk : (block + 1) * chunk])
        return total

    def part_copy(side, r, slot):
        return pltpu.make_async_remote_copy(
            src_ref=part_out.at[side, r], dst_ref=part_in.at[side, slot],
            send_sem=part_send.at[side, r], recv_sem=part_recv.at[side, slot],
            device_id=column(r), device_id_type=MESH,
        )

    for side in range(2):
        def foreign_here(step, _):
            place = around(step)
            foreign_copy(side, place, place).wait()
            return 0

        lax.fori_loop(0, m - 1, foreign_here, 0)
        for r in range(1, planes):
            part_out[side, r] = bag_sums(side, r).astype(BF16)
            part_copy(side, r, planes - r).start()

    choose(0)

    def near_here(step, _):
        place = around(step)
        near_copy(place, place).wait()
        return 0

    lax.fori_loop(0, m - 1, near_here, 0)
    for side in range(2):
        total = bag_sums(side, 0)
        for r in range(1, planes):
            part_copy(side, r, r).wait()
            total = total + part_in[side, r].astype(F32)
        columns = slice(side * half_width, (side + 1) * half_width)
        query_ref[:, columns] = total[:pairs].astype(BF16)
        item_ref[:, columns] = total[pairs:]


def lookup_scratch(grid, bags, pairs, table):
    ny, planes, cores = grid
    shard_rows, width = table.shape
    m = ny * cores
    cap = min(pairs, 3 * pairs * bags // (2 * m * planes))
    chunk = min(m * cap, 512)
    dma = pltpu.SemaphoreType.DMA
    return [
        pltpu.VMEM(table.shape, BF16),
        pltpu.VMEM(table.shape, F32),
        pltpu.VMEM((planes, bags, pairs), jnp.int32),
        pltpu.VMEM((128, pairs), F32),
        pltpu.VMEM((planes, pairs, 128), jnp.int32),
        pltpu.VMEM((m, planes, 2 * cap), jnp.int32),
        pltpu.VMEM((m, planes, 2 * cap), jnp.int32),
        pltpu.SMEM((m, planes, 2 * cap), jnp.int32),
        pltpu.VMEM((2, m, planes, cap, width // 2), BF16),
        pltpu.VMEM((2, planes, m, cap, width // 2), BF16),
        pltpu.VMEM((planes, m * cap // chunk, 2 * pairs, chunk), BF16),
        pltpu.VMEM((16, width), F32),
        pltpu.VMEM((2, planes, 2 * pairs, width // 2), BF16),
        pltpu.VMEM((2, planes, 2 * pairs, width // 2), BF16),
        dma((2,)),
        dma((planes,)),
        dma((planes,)),
        dma((m,)),
        dma((m,)),
        dma((3, m)),
        dma((3, m)),
        dma((2, planes)),
        dma((2, planes)),
    ]


def kernel(
    grid, nx, nz, owner_ref, row_ref, table_hbm, first_hbm, second_hbm, loss_ref, item_grad_ref, query_grad_ref,
    query_ref, item_ref, first, second, slope, items, queries, exps, total_out, total_in,
    query_out, query_in, item_sum, item_out, item_in, acc,
    local_sem, send_sem, recv_sem, *lookup_refs,
):
    blk = lax.axis_index("blk")
    x, z = blk // nz, blk % nz
    pairs, width = query_ref.shape
    steps, chunk = slope.shape[0], slope.shape[2]

    load_first = pltpu.make_async_copy(first_hbm, first, local_sem.at[0])
    load_second = pltpu.make_async_copy(second_hbm, second, local_sem.at[1])
    load_first.start()
    load_second.start()

    def along_x(step):
        there = lax.rem(x + step, nx)
        return there, there * nz + z

    def along_z(step):
        there = lax.rem(z + step, nz)
        return there, x * nz + there

    def meet(barrier):
        for axis, count in ((along_x, nx), (along_z, nz)):
            for step in range(1, count):
                pl.semaphore_signal(
                    barrier, inc=1, device_id={"blk": axis(step)[1]}, device_id_type=MESH
                )
        return nx + nz - 2

    lookup(grid, meet, owner_ref, row_ref, table_hbm, query_ref, item_ref, lookup_refs)
    item_unit, item_scale = unit_rows(item_ref[...])
    items[z] = item_unit.astype(BF16)

    def copy(phase, source, target, landing, step, axis):
        there, device = axis(step)
        return pltpu.make_async_remote_copy(
            src_ref=source, dst_ref=target,
            send_sem=send_sem.at[phase, there], recv_sem=recv_sem.at[phase, landing],
            device_id={"blk": device}, device_id_type=MESH,
        )

    def item_copy(step, slot):
        return copy(0, items.at[z], items.at[slot], slot, step, along_z)

    def query_copy(step, slot):
        return copy(1, queries.at[x], queries.at[slot], slot, step, along_x)

    def total_copy(step, slot):
        return copy(2, total_out, total_in.at[slot], slot, step, along_x)

    def query_sum_copy(step, slot):
        there = along_x(step)[0]
        return copy(3, query_out.at[there], query_in.at[slot], slot, step, along_x)

    def item_sum_copy(step, slot):
        there = along_z(step)[0]
        return copy(4, item_out.at[there], item_in.at[slot], slot, step, along_z)

    for step in range(1, nz):
        item_copy(step, z).start()

    acc[...] = jnp.zeros_like(acc)
    load_first.wait()
    load_second.wait()

    def forward(part, _):
        at = pl.ds(pl.multiple_of(part * chunk, chunk), chunk)
        pre = dot(query_ref[...], first[:, at])
        sigma = 0.5 + 0.5 * jnp.tanh(0.5 * pre)
        slope[part] = sigma * (1.0 + pre * (1.0 - sigma))
        acc[...] += dot((pre * sigma).astype(BF16), second[at, :])
        return 0

    lax.fori_loop(0, steps, forward, 0)
    query_unit, query_scale = unit_rows(acc[...])
    queries[x] = query_unit.astype(BF16)
    for step in range(1, nx):
        query_copy(step, x).start()

    diagonal = lax.broadcasted_iota(jnp.int32, (pairs, pairs), 0) == lax.broadcasted_iota(
        jnp.int32, (pairs, pairs), 1
    )

    own = None
    for step in range(nx):
        xi = along_x(step)[0]
        if step > 0:
            query_copy(step, xi).wait_recv()
        part = jnp.zeros((1, pairs), F32)
        for turn in range(nz):
            zi = along_z(turn)[0]
            if step == 0 and turn > 0:
                item_copy(turn, zi).wait_recv()
            scores = INV_TEMP * row_dot(items[zi], queries[xi])
            if step == 0 and turn == 0:
                own = jnp.sum(jnp.where(diagonal, scores, 0.0), axis=0, keepdims=True)
            value = jnp.exp(scores)
            exps[step, zi] = value
            part = part + jnp.sum(value, axis=0, keepdims=True)
        total_out[xi] = part
    total_in[x] = total_out[...]
    for step in range(1, nx):
        total_copy(step, x).start()
    for step in range(1, nx):
        total_copy(step, along_x(step)[0]).wait_recv()

    all_items = items[...].reshape(nz * pairs, width)
    query_sum = None
    for turn in range(nx):
        step = (turn + 1) % nx
        xi = along_x(step)[0]
        total = jnp.zeros((1, pairs), F32)
        for source in range(nx):
            total = total + total_in[source, xi]
        if step == 0:
            loss_ref[...] = jnp.log(total) - own
        prob = (exps[step].reshape(nz * pairs, pairs) * (1.0 / total)).astype(BF16)
        part = col_dot(prob, all_items)
        if step == 0:
            query_sum = part
        else:
            query_out[xi] = part.astype(BF16)
            query_sum_copy(step, x).start()
        added = dot(prob, queries[xi]).reshape(nz, pairs, width)
        item_sum[...] = added if turn == 0 else item_sum[...] + added
    for step in range(1, nz):
        zi = along_z(step)[0]
        item_out[zi] = item_sum[zi].astype(BF16)
        item_sum_copy(step, z).start()

    for step in range(1, nx):
        xi = along_x(step)[0]
        query_sum_copy(step, xi).wait_recv()
        query_sum = query_sum + query_in[xi].astype(F32)
    query_unit_grad = INV_TEMP * (query_sum - items[z].astype(F32))
    query_unit = acc[...] * query_scale
    out_grad = unit_backward(query_unit_grad, query_unit, query_scale).astype(BF16)
    acc[...] = jnp.zeros_like(acc)

    def backward(part, _):
        at = pl.ds(pl.multiple_of(part * chunk, chunk), chunk)
        hidden_grad = (row_dot(out_grad, second[at, :]) * slope[part]).astype(BF16)
        acc[...] += row_dot(hidden_grad, first[:, at])
        return 0

    lax.fori_loop(0, steps, backward, 0)
    query_grad_ref[...] = acc[...]

    total_items = item_sum[z]
    for step in range(1, nz):
        zi = along_z(step)[0]
        item_sum_copy(step, zi).wait_recv()
        total_items = total_items + item_in[zi].astype(F32)
    item_unit_grad = INV_TEMP * (total_items - queries[x].astype(F32))
    item_unit, item_scale = unit_rows(item_ref[...])
    item_grad_ref[...] = unit_backward(item_unit_grad, item_unit, item_scale)

    for step in range(1, nz):
        item_copy(step, z).wait_send()
        item_sum_copy(step, z).wait_send()
    for step in range(1, nx):
        query_copy(step, x).wait_send()
        total_copy(step, x).wait_send()
        query_sum_copy(step, x).wait_send()


def local(grid, nx, nz, id_table, w_first, w_second, owner_ids, row_ids):
    pairs, bags = owner_ids.shape
    width, hidden = w_first.shape
    chunk = min(hidden, 512)
    vmem = pl.BlockSpec(memory_space=pltpu.VMEM)
    hbm = pl.BlockSpec(memory_space=pltpu.HBM)
    most = max(nx, nz)
    loss, item_grad, query_grad = pl.pallas_call(
        functools.partial(kernel, grid, nx, nz),
        out_shape=(
            jax.ShapeDtypeStruct((1, pairs), F32),
            jax.ShapeDtypeStruct((pairs, width), F32),
            jax.ShapeDtypeStruct((pairs, width), F32),
        ),
        in_specs=[vmem, vmem, hbm, hbm, hbm],
        out_specs=(vmem, vmem, vmem),
        scratch_shapes=[
            pltpu.VMEM((pairs, width), BF16),
            pltpu.VMEM((pairs, width), F32),
            pltpu.VMEM(w_first.shape, BF16),
            pltpu.VMEM(w_second.shape, BF16),
            pltpu.VMEM((hidden // chunk, pairs, chunk), F32),
            pltpu.VMEM((nz, pairs, width), BF16),
            pltpu.VMEM((nx, pairs, width), BF16),
            pltpu.VMEM((nx, nz, pairs, pairs), F32),
            pltpu.VMEM((nx, 1, pairs), F32),
            pltpu.VMEM((nx, nx, 1, pairs), F32),
            pltpu.VMEM((nx, pairs, width), BF16),
            pltpu.VMEM((nx, pairs, width), BF16),
            pltpu.VMEM((nz, pairs, width), F32),
            pltpu.VMEM((nz, pairs, width), BF16),
            pltpu.VMEM((nz, pairs, width), BF16),
            pltpu.VMEM((pairs, width), F32),
            pltpu.SemaphoreType.DMA((2,)),
            pltpu.SemaphoreType.DMA((5, most)),
            pltpu.SemaphoreType.DMA((5, most)),
            *lookup_scratch(grid, bags, pairs, id_table),
        ],
        compiler_params=pltpu.CompilerParams(
            collective_id=0, has_side_effects=True, vmem_limit_bytes=60 * 2**20
        ),
        name="step",
    )(owner_ids.T, row_ids.T, id_table, w_first, w_second)
    return loss.reshape(-1), item_grad, query_grad


def solution(mesh):
    blocks, shards = mesh.shape["blk"], mesh.shape["table"]
    nx = math.isqrt(blocks)
    nz = blocks // nx
    grid = (shards // 6, 3, 2)
    placed = (P("table", None), P(), P(), P(("blk", "table"), None), P(("blk", "table"), None))
    return jax.shard_map(
        functools.partial(local, grid, nx, nz),
        mesh=mesh,
        in_specs=placed,
        out_specs=(P(("blk", "table")), P(("blk", "table"), None), P(("blk", "table"), None)),
        check_vma=False,
    )
```

```python
import functools
import math

import jax
import jax.numpy as jnp
from jax import lax
from jax.experimental import pallas as pl
from jax.experimental.pallas import tpu as pltpu
from jax.sharding import PartitionSpec as P

EPS = 1e-06
INV_TEMP = 20.0
MESH = pl.DeviceIdType.MESH
F32 = jnp.float32
BF16 = jnp.bfloat16


def row_dot(left, right):
    return lax.dot_general(left, right, (((1,), (1,)), ((), ())), preferred_element_type=F32)


def col_dot(left, right):
    return lax.dot_general(left, right, (((0,), (0,)), ((), ())), preferred_element_type=F32)


def dot(left, right):
    return jnp.dot(left, right, preferred_element_type=F32)


def unit_rows(vectors):
    scale = lax.rsqrt(jnp.sum(vectors * vectors, axis=-1, keepdims=True) + EPS)
    return vectors * scale, scale


def unit_backward(grad, unit, scale):
    return scale * (grad - unit * jnp.sum(unit * grad, axis=-1, keepdims=True))


def lookup(grid, meet, owner_ref, row_ref, table_ref, refs):
    ny, planes, cores = grid
    (table_bf, table_wide, ids, code_rows, codes, req_all, req_out, req_in, req_smem, rows_out, rows_in, select,
     stage, part_out, part_in, local_sem, ids_send, ids_recv, req_send, req_recv, rows_send, rows_recv,
     part_send, part_recv) = refs
    bags, pairs = owner_ref.shape
    shard_rows, width = table_ref.shape
    cap, half_width = rows_in.shape[3:]
    chunks, chunk = select.shape[1], select.shape[3]
    step_rows = stage.shape[0]
    half = bags // 2
    m = ny * cores
    n = m * planes
    t = lax.axis_index("table")
    plane = (t // cores) % planes
    q = t // (planes * cores) * cores + t % cores

    def shard(place, where):
        return place // cores * (planes * cores) + where * cores + place % cores

    def column(r):
        return {"table": shard(q, lax.rem(plane + r, planes))}

    def across(place):
        return {"table": shard(place, plane)}

    def around(step):
        away = m // 2 - (step + 1) // 2
        return lax.rem(q + away + (step % 2) * (m - 2 * away), m)

    def further(step):
        return lax.rem(t + step, n)

    fetch = pltpu.make_async_copy(table_ref, table_bf, local_sem.at[0])
    fetch.start()
    barrier = pltpu.get_barrier_semaphore()

    def greet(step, _):
        pl.semaphore_signal(barrier, inc=1, device_id={"table": further(step)}, device_id_type=MESH)
        return 0

    lax.fori_loop(1, n, greet, 0)
    others = meet(barrier)

    shard_iota = lax.broadcasted_iota(jnp.int32, (n, pairs), 0)
    shard_place = shard_iota // (planes * cores) * cores + shard_iota % cores
    first_slot = ((shard_iota // cores % planes * m + shard_place) * cap).astype(F32)
    digit_iota = lax.broadcasted_iota(jnp.int32, (2 * cap, pairs), 0)
    low_digit = digit_iota >= cap
    digit_slot = jnp.where(low_digit, digit_iota - cap, digit_iota).astype(F32)
    earlier = jnp.where(
        lax.broadcasted_iota(jnp.int32, (pairs, pairs), 0)
        < lax.broadcasted_iota(jnp.int32, (pairs, pairs), 1),
        1.0, 0.0,
    ).astype(BF16)
    count = jnp.zeros((n, 1), F32)
    wanted = jnp.zeros((n, 2 * cap), F32)
    for k in range(bags):
        hot = jnp.where(owner_ref[k : k + 1, :] == shard_iota, 1.0, 0.0)
        hot_bf = hot.astype(BF16)
        held = dot(hot_bf, earlier) + count
        slot = jnp.sum(hot * held, axis=0, keepdims=True)
        code = slot + jnp.sum(hot * first_slot, axis=0, keepdims=True)
        ids[0, k : k + 1, :] = code.astype(jnp.int32)
        row = row_ref[k : k + 1, :]
        digit = jnp.where(low_digit, row & 127, row >> 7).astype(F32)
        digit = jnp.where(digit_slot == slot, digit, 0.0).astype(BF16)
        wanted = wanted + row_dot(hot_bf, digit)
        count = count + jnp.sum(hot, axis=1, keepdims=True)
    req_all[...] = (wanted * 128.0 + pltpu.roll(wanted, cap, 1)).astype(jnp.int32)

    def split(place, _):
        req_out[place] = req_all[pl.ds(place, 1), :]
        return 0

    lax.fori_loop(0, n, split, 0)
    req_in[t] = req_out[t]
    pl.semaphore_wait(barrier, n - 1 + others)

    def request(to, slot):
        return pltpu.make_async_remote_copy(
            src_ref=req_out.at[to], dst_ref=req_in.at[slot],
            send_sem=req_send.at[to], recv_sem=req_recv.at[slot],
            device_id={"table": to}, device_id_type=MESH,
        )

    def ask(step, _):
        request(further(step), t).start()
        return 0

    lax.fori_loop(1, n, ask, 0)

    def ids_copy(r, slot):
        return pltpu.make_async_remote_copy(
            src_ref=ids.at[0], dst_ref=ids.at[slot], send_sem=ids_send.at[r], recv_sem=ids_recv.at[slot],
            device_id=column(r), device_id_type=MESH,
        )

    for r in range(1, planes):
        ids_copy(r, planes - r).start()

    fetch.wait()
    blocks = 32
    block_rows = shard_rows // blocks

    def widen(block, _):
        at = pl.ds(pl.multiple_of(block * block_rows, block_rows), block_rows)
        table_wide[at, :] = table_bf[at, :].astype(F32)
        return 0

    lax.fori_loop(0, blocks, widen, 0)

    def asked(step, _):
        request(further(step), further(step)).wait()
        return 0

    lax.fori_loop(1, n, asked, 0)
    to_smem = pltpu.make_async_copy(req_in, req_smem, local_sem.at[1])
    to_smem.start()
    to_smem.wait()

    def gather(place, r, left, right):
        asker = shard(place, lax.rem(plane + r, planes))

        def some(part, _):
            for s in range(step_rows):
                index = req_smem[asker, 0, part * step_rows + s] & (shard_rows - 1)
                stage[s : s + 1, :] = table_wide[pl.ds(index, 1), :]
            at = pl.ds(pl.multiple_of(part * step_rows, step_rows), step_rows)
            rows = stage[...].astype(BF16)
            left[at, :] = rows[:, :half_width]
            right[at, :] = rows[:, half_width:]
            return 0

        lax.fori_loop(0, cap // step_rows, some, 0)

    foreign = pl.ds(1, planes - 1)

    def foreign_copy(side, place, slot):
        return pltpu.make_async_remote_copy(
            src_ref=rows_out.at[side, place, foreign], dst_ref=rows_in.at[side, foreign, slot],
            send_sem=rows_send.at[side, place], recv_sem=rows_recv.at[side, slot],
            device_id=across(place), device_id_type=MESH,
        )

    def near_copy(place, slot):
        return pltpu.make_async_remote_copy(
            src_ref=rows_out.at[:, place, 0], dst_ref=rows_in.at[:, 0, slot],
            send_sem=rows_send.at[2, place], recv_sem=rows_recv.at[2, slot],
            device_id=across(place), device_id_type=MESH,
        )

    def serve_foreign(step, _):
        place = around(step)
        for r in range(1, planes):
            gather(place, r, rows_out.at[0, place, r], rows_out.at[1, place, r])
        foreign_copy(0, place, q).start()
        return 0

    def serve_second(step, _):
        foreign_copy(1, around(step), q).start()
        return 0

    def collect_near(step, _):
        place = around(step)
        gather(place, 0, rows_out.at[0, place, 0], rows_out.at[1, place, 0])
        return 0

    def serve_near(step, _):
        near_copy(around(step), q).start()
        return 0

    lax.fori_loop(0, m - 1, serve_foreign, 0)
    lax.fori_loop(0, m - 1, serve_second, 0)
    for r in range(planes):
        gather(q, r, rows_in.at[0, r, q], rows_in.at[1, r, q])
    lax.fori_loop(0, m - 1, collect_near, 0)

    code_rows[...] = jnp.zeros_like(code_rows)

    def choose(r):
        code_rows[0:bags, :] = ids[r].astype(F32)
        codes[...] = jnp.transpose(code_rows[...]).astype(jnp.int32) - plane * (m * cap)

        def some(block, _):
            place = lax.broadcasted_iota(jnp.int32, (pairs, chunk), 1) + block * chunk
            for side in range(2):
                mask = codes[:, side * half : side * half + 1] == place
                for k in range(side * half + 1, (side + 1) * half):
                    mask = mask | (codes[:, k : k + 1] == place)
                select[r, block, side * pairs : (side + 1) * pairs, :] = jnp.where(mask, 1.0, 0.0).astype(BF16)
            return 0

        lax.fori_loop(0, chunks, some, 0)

    for r in range(1, planes):
        ids_copy(r, r).wait()
        choose(r)

    def bag_sums(side, r, bag):
        rows = rows_in[side, r].reshape(m * cap, half_width)
        at = slice(bag * pairs, (bag + 1) * pairs)
        total = dot(select[r, 0, at, :], rows[:chunk])
        for block in range(1, chunks):
            total = total + dot(select[r, block, at, :], rows[block * chunk : (block + 1) * chunk])
        return total

    def part_copy(side, r, bag, slot):
        return pltpu.make_async_remote_copy(
            src_ref=part_out.at[side, r, bag], dst_ref=part_in.at[side, slot, bag],
            send_sem=part_send.at[side, r, bag], recv_sem=part_recv.at[side, slot, bag],
            device_id=column(r), device_id_type=MESH,
        )

    for side in range(2):
        def foreign_here(step, _):
            place = around(step)
            foreign_copy(side, place, place).wait()
            return 0

        lax.fori_loop(0, m - 1, foreign_here, 0)
        if side == 0:
            lax.fori_loop(0, m - 1, serve_near, 0)
        for bag in (1, 0):
            for r in range(1, planes):
                part_out[side, r, bag] = bag_sums(side, r, bag).astype(BF16)
                part_copy(side, r, bag, planes - r).start()

    choose(0)

    def near_here(step, _):
        place = around(step)
        near_copy(place, place).wait()
        return 0

    lax.fori_loop(0, m - 1, near_here, 0)

    def finish(bag, target):
        for side in range(2):
            total = bag_sums(side, 0, bag)
            for r in range(1, planes):
                part_copy(side, r, bag, r).wait()
                total = total + part_in[side, r, bag].astype(F32)
            target[:, side * half_width : (side + 1) * half_width] = total.astype(target.dtype)

    return finish


def lookup_scratch(grid, bags, pairs, table):
    ny, planes, cores = grid
    shard_rows, width = table.shape
    m = ny * cores
    cap = min(pairs, 3 * pairs * bags // (2 * m * planes))
    chunk = min(m * cap, 512)
    dma = pltpu.SemaphoreType.DMA
    return [
        pltpu.VMEM(table.shape, BF16),
        pltpu.VMEM(table.shape, F32),
        pltpu.VMEM((planes, bags, pairs), jnp.int32),
        pltpu.VMEM((128, pairs), F32),
        pltpu.VMEM((pairs, 128), jnp.int32),
        pltpu.VMEM((m * planes, 2 * cap), jnp.int32),
        pltpu.VMEM((m * planes, 1, 2 * cap), jnp.int32),
        pltpu.VMEM((m * planes, 1, 2 * cap), jnp.int32),
        pltpu.SMEM((m * planes, 1, 2 * cap), jnp.int32),
        pltpu.VMEM((2, m, planes, cap, width // 2), BF16),
        pltpu.VMEM((2, planes, m, cap, width // 2), BF16),
        pltpu.VMEM((planes, m * cap // chunk, 2 * pairs, chunk), BF16),
        pltpu.VMEM((16, width), F32),
        pltpu.VMEM((2, planes, 2, pairs, width // 2), BF16),
        pltpu.VMEM((2, planes, 2, pairs, width // 2), BF16),
        dma((2,)),
        dma((planes,)),
        dma((planes,)),
        dma((m * planes,)),
        dma((m * planes,)),
        dma((3, m)),
        dma((3, m)),
        dma((2, planes, 2)),
        dma((2, planes, 2)),
    ]


def kernel(
    grid, nx, nz, owner_ref, row_ref, table_hbm, first_hbm, second_hbm, loss_ref, item_grad_ref, query_grad_ref,
    query_ref, item_ref, first, second, slope, items, queries, exps, total_out, total_in,
    query_out, query_in, probs, item_sum, item_out, item_in, acc,
    local_sem, send_sem, recv_sem, *lookup_refs,
):
    blk = lax.axis_index("blk")
    x, z = blk // nz, blk % nz
    pairs, width = query_ref.shape
    steps, chunk = slope.shape[0], slope.shape[2]

    load_first = pltpu.make_async_copy(first_hbm, first, local_sem.at[0])
    load_second = pltpu.make_async_copy(second_hbm, second, local_sem.at[1])
    load_first.start()
    load_second.start()

    def along_x(step):
        there = lax.rem(x + step, nx)
        return there, there * nz + z

    def along_z(step):
        there = lax.rem(z + step, nz)
        return there, x * nz + there

    def meet(barrier):
        for axis, count in ((along_x, nx), (along_z, nz)):
            for step in range(1, count):
                pl.semaphore_signal(
                    barrier, inc=1, device_id={"blk": axis(step)[1]}, device_id_type=MESH
                )
        return nx + nz - 2

    finish = lookup(grid, meet, owner_ref, row_ref, table_hbm, lookup_refs)
    finish(1, item_ref)
    item_unit, item_scale = unit_rows(item_ref[...])
    items[z] = item_unit.astype(BF16)

    def copy(phase, source, target, landing, step, axis):
        there, device = axis(step)
        return pltpu.make_async_remote_copy(
            src_ref=source, dst_ref=target,
            send_sem=send_sem.at[phase, there], recv_sem=recv_sem.at[phase, landing],
            device_id={"blk": device}, device_id_type=MESH,
        )

    def item_copy(step, slot):
        return copy(0, items.at[z], items.at[slot], slot, step, along_z)

    def query_copy(step, slot):
        return copy(1, queries.at[x], queries.at[slot], slot, step, along_x)

    def total_copy(step, slot):
        return copy(2, total_out, total_in.at[slot], slot, step, along_x)

    def query_sum_copy(step, slot):
        there = along_x(step)[0]
        return copy(3, query_out.at[there], query_in.at[slot], slot, step, along_x)

    def item_sum_copy(step, slot):
        there = along_z(step)[0]
        return copy(4, item_out.at[there], item_in.at[slot], slot, step, along_z)

    for step in range(1, nz):
        item_copy(step, z).start()

    finish(0, query_ref)
    acc[...] = jnp.zeros_like(acc)
    load_first.wait()
    load_second.wait()

    def forward(part, _):
        at = pl.ds(pl.multiple_of(part * chunk, chunk), chunk)
        pre = dot(query_ref[...], first[:, at])
        sigma = 0.5 + 0.5 * jnp.tanh(0.5 * pre)
        slope[part] = sigma * (1.0 + pre * (1.0 - sigma))
        acc[...] += dot((pre * sigma).astype(BF16), second[at, :])
        return 0

    lax.fori_loop(0, steps, forward, 0)
    query_unit, query_scale = unit_rows(acc[...])
    queries[x] = query_unit.astype(BF16)
    for step in range(1, nx):
        query_copy(step, x).start()

    diagonal = lax.broadcasted_iota(jnp.int32, (pairs, pairs), 0) == lax.broadcasted_iota(
        jnp.int32, (pairs, pairs), 1
    )

    own = None
    for step in range(nx):
        xi = along_x(step)[0]
        if step > 0:
            query_copy(step, xi).wait_recv()
        part = jnp.zeros((1, pairs), F32)
        for turn in range(nz):
            zi = along_z(turn)[0]
            if step == 0 and turn > 0:
                item_copy(turn, zi).wait_recv()
            scores = INV_TEMP * row_dot(items[zi], queries[xi])
            if step == 0 and turn == 0:
                own = jnp.sum(jnp.where(diagonal, scores, 0.0), axis=0, keepdims=True)
            value = jnp.exp(scores)
            exps[step, zi] = value
            part = part + jnp.sum(value, axis=0, keepdims=True)
        total_out[xi] = part
    total_in[x] = total_out[...]
    for step in range(1, nx):
        total_copy(step, x).start()
    for step in range(1, nx):
        total_copy(step, along_x(step)[0]).wait_recv()

    for step in range(nx):
        xi = along_x(step)[0]
        total = jnp.zeros((1, pairs), F32)
        for source in range(nx):
            total = total + total_in[source, xi]
        if step == 0:
            loss_ref[...] = jnp.log(total) - own
        probs[step] = (exps[step] * (1.0 / total)).astype(BF16)

    def item_part(zi):
        part = dot(probs[0, zi], queries[x])
        for step in range(1, nx):
            part = part + dot(probs[step, zi], queries[along_x(step)[0]])
        return part

    def query_part(step):
        return col_dot(probs[step].reshape(nz * pairs, pairs), items[...].reshape(nz * pairs, width))

    for step in range(1, nz):
        zi = along_z(step)[0]
        item_out[zi] = item_part(zi).astype(BF16)
        item_sum_copy(step, z).start()
    for step in range(1, nx):
        query_out[along_x(step)[0]] = query_part(step).astype(BF16)
        query_sum_copy(step, x).start()
    query_sum = query_part(0)
    item_sum[...] = item_part(z)

    for step in range(1, nx):
        xi = along_x(step)[0]
        query_sum_copy(step, xi).wait_recv()
        query_sum = query_sum + query_in[xi].astype(F32)
    query_unit_grad = INV_TEMP * (query_sum - items[z].astype(F32))
    query_unit = acc[...] * query_scale
    out_grad = unit_backward(query_unit_grad, query_unit, query_scale).astype(BF16)
    acc[...] = jnp.zeros_like(acc)

    def backward(part, _):
        at = pl.ds(pl.multiple_of(part * chunk, chunk), chunk)
        hidden_grad = (row_dot(out_grad, second[at, :]) * slope[part]).astype(BF16)
        acc[...] += row_dot(hidden_grad, first[:, at])
        return 0

    lax.fori_loop(0, steps, backward, 0)
    query_grad_ref[...] = acc[...]

    total_items = item_sum[...]
    for step in range(1, nz):
        zi = along_z(step)[0]
        item_sum_copy(step, zi).wait_recv()
        total_items = total_items + item_in[zi].astype(F32)
    item_unit_grad = INV_TEMP * (total_items - queries[x].astype(F32))
    item_unit, item_scale = unit_rows(item_ref[...])
    item_grad_ref[...] = unit_backward(item_unit_grad, item_unit, item_scale)

    for step in range(1, nz):
        item_copy(step, z).wait_send()
        item_sum_copy(step, z).wait_send()
    for step in range(1, nx):
        query_copy(step, x).wait_send()
        total_copy(step, x).wait_send()
        query_sum_copy(step, x).wait_send()


def local(grid, nx, nz, id_table, w_first, w_second, owner_ids, row_ids):
    pairs, bags = owner_ids.shape
    width, hidden = w_first.shape
    chunk = min(hidden, 512)
    vmem = pl.BlockSpec(memory_space=pltpu.VMEM)
    hbm = pl.BlockSpec(memory_space=pltpu.HBM)
    most = max(nx, nz)
    loss, item_grad, query_grad = pl.pallas_call(
        functools.partial(kernel, grid, nx, nz),
        out_shape=(
            jax.ShapeDtypeStruct((1, pairs), F32),
            jax.ShapeDtypeStruct((pairs, width), F32),
            jax.ShapeDtypeStruct((pairs, width), F32),
        ),
        in_specs=[vmem, vmem, hbm, hbm, hbm],
        out_specs=(vmem, vmem, vmem),
        scratch_shapes=[
            pltpu.VMEM((pairs, width), BF16),
            pltpu.VMEM((pairs, width), F32),
            pltpu.VMEM(w_first.shape, BF16),
            pltpu.VMEM(w_second.shape, BF16),
            pltpu.VMEM((hidden // chunk, pairs, chunk), F32),
            pltpu.VMEM((nz, pairs, width), BF16),
            pltpu.VMEM((nx, pairs, width), BF16),
            pltpu.VMEM((nx, nz, pairs, pairs), F32),
            pltpu.VMEM((nx, 1, pairs), F32),
            pltpu.VMEM((nx, nx, 1, pairs), F32),
            pltpu.VMEM((nx, pairs, width), BF16),
            pltpu.VMEM((nx, pairs, width), BF16),
            pltpu.VMEM((nx, nz, pairs, pairs), BF16),
            pltpu.VMEM((pairs, width), F32),
            pltpu.VMEM((nz, pairs, width), BF16),
            pltpu.VMEM((nz, pairs, width), BF16),
            pltpu.VMEM((pairs, width), F32),
            pltpu.SemaphoreType.DMA((2,)),
            pltpu.SemaphoreType.DMA((5, most)),
            pltpu.SemaphoreType.DMA((5, most)),
            *lookup_scratch(grid, bags, pairs, id_table),
        ],
        compiler_params=pltpu.CompilerParams(
            collective_id=0, has_side_effects=True, vmem_limit_bytes=52 * 2**20
        ),
        name="step",
    )(owner_ids.T, row_ids.T, id_table, w_first, w_second)
    return loss.reshape(-1), item_grad, query_grad


def solution(mesh):
    blocks, shards = mesh.shape["blk"], mesh.shape["table"]
    nx = math.isqrt(blocks)
    nz = blocks // nx
    grid = (shards // 6, 3, 2)
    placed = (P("table", None), P(), P(), P(("blk", "table"), None), P(("blk", "table"), None))
    return jax.shard_map(
        functools.partial(local, grid, nx, nz),
        mesh=mesh,
        in_specs=placed,
        out_specs=(P(("blk", "table")), P(("blk", "table"), None), P(("blk", "table"), None)),
        check_vma=False,
    )
```

```python
import functools
import math

import jax
import jax.numpy as jnp
from jax import lax
from jax.experimental import pallas as pl
from jax.experimental.pallas import tpu as pltpu
from jax.sharding import PartitionSpec as P

EPS = 1e-06
INV_TEMP = 20.0
MESH = pl.DeviceIdType.MESH
F32 = jnp.float32
BF16 = jnp.bfloat16


def row_dot(left, right):
    return lax.dot_general(left, right, (((1,), (1,)), ((), ())), preferred_element_type=F32)


def col_dot(left, right):
    return lax.dot_general(left, right, (((0,), (0,)), ((), ())), preferred_element_type=F32)


def dot(left, right):
    return jnp.dot(left, right, preferred_element_type=F32)


def unit_rows(vectors):
    scale = lax.rsqrt(jnp.sum(vectors * vectors, axis=-1, keepdims=True) + EPS)
    return vectors * scale, scale


def unit_backward(grad, unit, scale):
    return scale * (grad - unit * jnp.sum(unit * grad, axis=-1, keepdims=True))


def lookup(grid, meet, packed_ref, table_ref, refs):
    ny, planes, cores = grid
    (table_bf, table_wide, ids, code_rows, codes, req_all, req_out, req_in, req_smem, rows_out, rows_in, select,
     stage, part_out, part_in, local_sem, ids_send, ids_recv, req_send, req_recv, rows_send, rows_recv,
     part_send, part_recv, smem_sem) = refs
    bags, pairs = packed_ref.shape
    shard_rows, width = table_ref.shape
    cap, half_width = rows_in.shape[3:]
    chunks, chunk = select.shape[1], select.shape[3]
    step_rows = stage.shape[0]
    half = bags // 2
    m = ny * cores
    n = m * planes
    t = lax.axis_index("table")
    plane = (t // cores) % planes
    q = t // (planes * cores) * cores + t % cores

    def shard(place, where):
        return place // cores * (planes * cores) + where * cores + place % cores

    def column(r):
        return {"table": shard(q, lax.rem(plane + r, planes))}

    def across(place):
        return {"table": shard(place, plane)}

    def around(step):
        away = m // 2 - (step + 1) // 2
        return lax.rem(q + away + (step % 2) * (m - 2 * away), m)

    def asker(place, r):
        return shard(place, lax.rem(plane + r, planes))

    fetch = pltpu.make_async_copy(table_ref, table_bf, local_sem.at[0])
    fetch.start()
    barrier = pltpu.get_barrier_semaphore()

    def greet(step, _):
        other = lax.rem(t + step, n)
        pl.semaphore_signal(barrier, inc=1, device_id={"table": other}, device_id_type=MESH)
        return 0

    lax.fori_loop(1, n, greet, 0)
    others = meet(barrier)

    shard_iota = lax.broadcasted_iota(jnp.int32, (n, pairs), 0)
    shard_place = shard_iota // (planes * cores) * cores + shard_iota % cores
    first_slot = ((shard_iota // cores % planes * m + shard_place) * cap).astype(F32)
    digit_iota = lax.broadcasted_iota(jnp.int32, (2 * cap, pairs), 0)
    low_digit = digit_iota >= cap
    digit_slot = jnp.where(low_digit, digit_iota - cap, digit_iota).astype(F32)
    earlier = jnp.where(
        lax.broadcasted_iota(jnp.int32, (pairs, pairs), 0)
        < lax.broadcasted_iota(jnp.int32, (pairs, pairs), 1),
        1.0, 0.0,
    ).astype(BF16)
    bits = shard_rows.bit_length() - 1
    count = jnp.zeros((n, 1), F32)
    wanted = jnp.zeros((n, 2 * cap), F32)
    for k in range(bags):
        packed = packed_ref[k : k + 1, :]
        hot = jnp.where(packed >> bits == shard_iota, 1.0, 0.0)
        hot_bf = hot.astype(BF16)
        held = dot(hot_bf, earlier) + count
        slot = jnp.sum(hot * held, axis=0, keepdims=True)
        code = slot + jnp.sum(hot * first_slot, axis=0, keepdims=True)
        ids[0, k : k + 1, :] = code.astype(jnp.int32)
        digit = jnp.where(low_digit, packed & 127, (packed & (shard_rows - 1)) >> 7).astype(F32)
        digit = jnp.where(digit_slot == slot, digit, 0.0).astype(BF16)
        wanted = wanted + row_dot(hot_bf, digit)
        count = count + jnp.sum(hot, axis=1, keepdims=True)
    req_all[...] = (wanted * 128.0 + pltpu.roll(wanted, cap, 1)).astype(jnp.int32)

    def split(place, _):
        req_out[place] = req_all[pl.ds(place, 1), :]
        return 0

    lax.fori_loop(0, n, split, 0)
    pl.semaphore_wait(barrier, n - 1 + others)

    def request(place, r, slot, slot_r):
        to = asker(place, r)
        return pltpu.make_async_remote_copy(
            src_ref=req_out.at[to], dst_ref=req_in.at[slot, slot_r],
            send_sem=req_send.at[place, r], recv_sem=req_recv.at[slot, slot_r],
            device_id={"table": to}, device_id_type=MESH,
        )

    def ask(step, _):
        for r in (*range(1, planes), 0):
            request(around(step), r, q, (planes - r) % planes).start()
        return 0

    lax.fori_loop(0, m - 1, ask, 0)
    for r in range(1, planes):
        request(q, r, q, planes - r).start()
    req_in[q, 0] = req_out[t]

    def ids_copy(r, slot):
        return pltpu.make_async_remote_copy(
            src_ref=ids.at[0], dst_ref=ids.at[slot], send_sem=ids_send.at[r], recv_sem=ids_recv.at[slot],
            device_id=column(r), device_id_type=MESH,
        )

    for r in range(1, planes):
        ids_copy(r, planes - r).start()

    fetch.wait()
    blocks = 32
    block_rows = shard_rows // blocks

    def widen(block, _):
        at = pl.ds(pl.multiple_of(block * block_rows, block_rows), block_rows)
        table_wide[at, :] = table_bf[at, :].astype(F32)
        return 0

    lax.fori_loop(0, blocks, widen, 0)

    def to_smem(place):
        return pltpu.make_async_copy(req_in.at[place], req_smem.at[place], smem_sem.at[place])

    def asked(place):
        for r in range(planes):
            request(place, r, place, r).wait()
        to_smem(place).start()

    def gather(place, r, left, right):
        def some(part, _):
            for s in range(step_rows):
                index = req_smem[place, r, 0, part * step_rows + s] & (shard_rows - 1)
                stage[s : s + 1, :] = table_wide[pl.ds(index, 1), :]
            at = pl.ds(pl.multiple_of(part * step_rows, step_rows), step_rows)
            rows = stage[...].astype(BF16)
            left[at, :] = rows[:, :half_width]
            right[at, :] = rows[:, half_width:]
            return 0

        lax.fori_loop(0, cap // step_rows, some, 0)

    foreign = pl.ds(1, planes - 1)

    def foreign_copy(side, place, slot):
        return pltpu.make_async_remote_copy(
            src_ref=rows_out.at[side, place, foreign], dst_ref=rows_in.at[side, foreign, slot],
            send_sem=rows_send.at[side, place], recv_sem=rows_recv.at[side, slot],
            device_id=across(place), device_id_type=MESH,
        )

    def near_copy(place, slot):
        return pltpu.make_async_remote_copy(
            src_ref=rows_out.at[:, place, 0], dst_ref=rows_in.at[:, 0, slot],
            send_sem=rows_send.at[2, place], recv_sem=rows_recv.at[2, slot],
            device_id=across(place), device_id_type=MESH,
        )

    def serve_foreign(step, _):
        place = around(step)

        @pl.when(step < m - 2)
        def _():
            asked(around(step + 1))

        to_smem(place).wait()
        for r in range(1, planes):
            gather(place, r, rows_out.at[0, place, r], rows_out.at[1, place, r])
        foreign_copy(0, place, q).start()
        return 0

    def serve_second(step, _):
        foreign_copy(1, around(step), q).start()
        return 0

    def collect_near(step, _):
        place = around(step)
        gather(place, 0, rows_out.at[0, place, 0], rows_out.at[1, place, 0])
        return 0

    def serve_near(step, _):
        near_copy(around(step), q).start()
        return 0

    asked(around(0))
    lax.fori_loop(0, m - 1, serve_foreign, 0)
    lax.fori_loop(0, m - 1, serve_second, 0)
    for r in range(1, planes):
        request(q, r, q, r).wait()
    to_smem(q).start()
    to_smem(q).wait()
    for r in range(planes):
        gather(q, r, rows_in.at[0, r, q], rows_in.at[1, r, q])
    lax.fori_loop(0, m - 1, collect_near, 0)

    code_rows[...] = jnp.zeros_like(code_rows)

    def choose(r):
        code_rows[0:bags, :] = ids[r].astype(F32)
        codes[...] = jnp.transpose(code_rows[...]).astype(jnp.int32) - plane * (m * cap)

        def some(block, _):
            place = lax.broadcasted_iota(jnp.int32, (pairs, chunk), 1) + block * chunk
            for side in range(2):
                mask = codes[:, side * half : side * half + 1] == place
                for k in range(side * half + 1, (side + 1) * half):
                    mask = mask | (codes[:, k : k + 1] == place)
                select[r, block, side * pairs : (side + 1) * pairs, :] = jnp.where(mask, 1.0, 0.0).astype(BF16)
            return 0

        lax.fori_loop(0, chunks, some, 0)

    for r in range(1, planes):
        ids_copy(r, r).wait()
        choose(r)

    def bag_sums(side, r, bag):
        rows = rows_in[side, r].reshape(m * cap, half_width)
        at = slice(bag * pairs, (bag + 1) * pairs)
        total = dot(select[r, 0, at, :], rows[:chunk])
        for block in range(1, chunks):
            total = total + dot(select[r, block, at, :], rows[block * chunk : (block + 1) * chunk])
        return total

    def part_copy(side, r, bag, slot):
        return pltpu.make_async_remote_copy(
            src_ref=part_out.at[side, r, bag], dst_ref=part_in.at[side, slot, bag],
            send_sem=part_send.at[side, r, bag], recv_sem=part_recv.at[side, slot, bag],
            device_id=column(r), device_id_type=MESH,
        )

    for side in range(2):
        def foreign_here(step, _):
            place = around(step)
            foreign_copy(side, place, place).wait()
            return 0

        if side == 1:
            lax.fori_loop(0, 2 * m // 3, foreign_here, 0)
            lax.fori_loop(0, m - 1, serve_near, 0)
            lax.fori_loop(2 * m // 3, m - 1, foreign_here, 0)
        else:
            lax.fori_loop(0, m - 1, foreign_here, 0)
        for bag in (1, 0):
            for r in range(1, planes):
                part_out[side, r, bag] = bag_sums(side, r, bag).astype(BF16)
                part_copy(side, r, bag, planes - r).start()

    choose(0)

    def near_here(step, _):
        place = around(step)
        near_copy(place, place).wait()
        return 0

    lax.fori_loop(0, m - 1, near_here, 0)

    def finish(bag, target):
        for side in range(2):
            total = bag_sums(side, 0, bag)
            for r in range(1, planes):
                part_copy(side, r, bag, r).wait()
                total = total + part_in[side, r, bag].astype(F32)
            target[:, side * half_width : (side + 1) * half_width] = total.astype(target.dtype)

    return finish


def lookup_scratch(grid, bags, pairs, table):
    ny, planes, cores = grid
    shard_rows, width = table.shape
    m = ny * cores
    cap = min(pairs, 3 * pairs * bags // (2 * m * planes))
    chunk = min(m * cap, 512)
    dma = pltpu.SemaphoreType.DMA
    return [
        pltpu.VMEM(table.shape, BF16),
        pltpu.VMEM(table.shape, F32),
        pltpu.VMEM((planes, bags, pairs), jnp.int32),
        pltpu.VMEM((128, pairs), F32),
        pltpu.VMEM((pairs, 128), jnp.int32),
        pltpu.VMEM((m * planes, 2 * cap), jnp.int32),
        pltpu.VMEM((m * planes, 1, 2 * cap), jnp.int32),
        pltpu.VMEM((m, planes, 1, 2 * cap), jnp.int32),
        pltpu.SMEM((m, planes, 1, 2 * cap), jnp.int32),
        pltpu.VMEM((2, m, planes, cap, width // 2), BF16),
        pltpu.VMEM((2, planes, m, cap, width // 2), BF16),
        pltpu.VMEM((planes, m * cap // chunk, 2 * pairs, chunk), BF16),
        pltpu.VMEM((16, width), F32),
        pltpu.VMEM((2, planes, 2, pairs, width // 2), BF16),
        pltpu.VMEM((2, planes, 2, pairs, width // 2), BF16),
        dma((2,)),
        dma((planes,)),
        dma((planes,)),
        dma((m, planes)),
        dma((m, planes)),
        dma((3, m)),
        dma((3, m)),
        dma((2, planes, 2)),
        dma((2, planes, 2)),
        dma((m,)),
    ]


def kernel(
    grid, nx, nz, packed_ref, table_hbm, first_hbm, second_hbm, loss_ref, item_grad_ref, query_grad_ref,
    query_ref, item_ref, first, second, slope, items, queries, exps, total_out, total_in,
    query_out, query_in, probs, item_sum, item_out, item_in, acc,
    local_sem, send_sem, recv_sem, *lookup_refs,
):
    blk = lax.axis_index("blk")
    x, z = blk // nz, blk % nz
    pairs, width = query_ref.shape
    steps, chunk = slope.shape[0], slope.shape[2]

    load_first = pltpu.make_async_copy(first_hbm, first, local_sem.at[0])
    load_second = pltpu.make_async_copy(second_hbm, second, local_sem.at[1])
    load_first.start()
    load_second.start()

    def along_x(step):
        there = lax.rem(x + step, nx)
        return there, there * nz + z

    def along_z(step):
        there = lax.rem(z + step, nz)
        return there, x * nz + there

    def meet(barrier):
        for axis, count in ((along_x, nx), (along_z, nz)):
            for step in range(1, count):
                pl.semaphore_signal(
                    barrier, inc=1, device_id={"blk": axis(step)[1]}, device_id_type=MESH
                )
        return nx + nz - 2

    finish = lookup(grid, meet, packed_ref, table_hbm, lookup_refs)
    finish(1, item_ref)
    item_unit, item_scale = unit_rows(item_ref[...])
    items[z] = item_unit.astype(BF16)

    def copy(phase, source, target, landing, step, axis):
        there, device = axis(step)
        return pltpu.make_async_remote_copy(
            src_ref=source, dst_ref=target,
            send_sem=send_sem.at[phase, there], recv_sem=recv_sem.at[phase, landing],
            device_id={"blk": device}, device_id_type=MESH,
        )

    def item_copy(step, slot):
        return copy(0, items.at[z], items.at[slot], slot, step, along_z)

    def query_copy(step, slot):
        return copy(1, queries.at[x], queries.at[slot], slot, step, along_x)

    def total_copy(step, slot):
        return copy(2, total_out, total_in.at[slot], slot, step, along_x)

    def query_sum_copy(step, slot):
        there = along_x(step)[0]
        return copy(3, query_out.at[there], query_in.at[slot], slot, step, along_x)

    def item_sum_copy(step, slot):
        there = along_z(step)[0]
        return copy(4, item_out.at[there], item_in.at[slot], slot, step, along_z)

    for step in range(1, nz):
        item_copy(step, z).start()

    finish(0, query_ref)
    acc[...] = jnp.zeros_like(acc)
    load_first.wait()
    load_second.wait()

    def forward(part, _):
        at = pl.ds(pl.multiple_of(part * chunk, chunk), chunk)
        pre = dot(query_ref[...], first[:, at])
        sigma = 0.5 + 0.5 * jnp.tanh(0.5 * pre)
        slope[part] = sigma * (1.0 + pre * (1.0 - sigma))
        acc[...] += dot((pre * sigma).astype(BF16), second[at, :])
        return 0

    lax.fori_loop(0, steps, forward, 0)
    query_unit, query_scale = unit_rows(acc[...])
    queries[x] = query_unit.astype(BF16)
    for step in range(1, nx):
        query_copy(step, x).start()

    diagonal = lax.broadcasted_iota(jnp.int32, (pairs, pairs), 0) == lax.broadcasted_iota(
        jnp.int32, (pairs, pairs), 1
    )

    own = None
    for step in range(nx):
        xi = along_x(step)[0]
        if step > 0:
            query_copy(step, xi).wait_recv()
        part = jnp.zeros((1, pairs), F32)
        for turn in range(nz):
            zi = along_z(turn)[0]
            if step == 0 and turn > 0:
                item_copy(turn, zi).wait_recv()
            scores = INV_TEMP * row_dot(items[zi], queries[xi])
            if step == 0 and turn == 0:
                own = jnp.sum(jnp.where(diagonal, scores, 0.0), axis=0, keepdims=True)
            value = jnp.exp(scores)
            exps[step, zi] = value
            part = part + jnp.sum(value, axis=0, keepdims=True)
        total_out[xi] = part
    total_in[x] = total_out[...]
    for step in range(1, nx):
        total_copy(step, x).start()
    for step in range(1, nx):
        total_copy(step, along_x(step)[0]).wait_recv()

    for step in range(nx):
        xi = along_x(step)[0]
        total = jnp.zeros((1, pairs), F32)
        for source in range(nx):
            total = total + total_in[source, xi]
        if step == 0:
            loss_ref[...] = jnp.log(total) - own
        probs[step] = (exps[step] * (1.0 / total)).astype(BF16)

    def item_part(zi):
        part = dot(probs[0, zi], queries[x])
        for step in range(1, nx):
            part = part + dot(probs[step, zi], queries[along_x(step)[0]])
        return part

    def query_part(step):
        return col_dot(probs[step].reshape(nz * pairs, pairs), items[...].reshape(nz * pairs, width))

    for step in range(1, nz):
        zi = along_z(step)[0]
        item_out[zi] = item_part(zi).astype(BF16)
        item_sum_copy(step, z).start()
    for step in range(1, nx):
        query_out[along_x(step)[0]] = query_part(step).astype(BF16)
        query_sum_copy(step, x).start()
    query_sum = query_part(0)
    item_sum[...] = item_part(z)

    for step in range(1, nx):
        xi = along_x(step)[0]
        query_sum_copy(step, xi).wait_recv()
        query_sum = query_sum + query_in[xi].astype(F32)
    query_unit_grad = INV_TEMP * (query_sum - items[z].astype(F32))
    query_unit = acc[...] * query_scale
    out_grad = unit_backward(query_unit_grad, query_unit, query_scale).astype(BF16)
    acc[...] = jnp.zeros_like(acc)

    def backward(part, _):
        at = pl.ds(pl.multiple_of(part * chunk, chunk), chunk)
        hidden_grad = (row_dot(out_grad, second[at, :]) * slope[part]).astype(BF16)
        acc[...] += row_dot(hidden_grad, first[:, at])
        return 0

    lax.fori_loop(0, steps, backward, 0)
    query_grad_ref[...] = acc[...]

    total_items = item_sum[...]
    for step in range(1, nz):
        zi = along_z(step)[0]
        item_sum_copy(step, zi).wait_recv()
        total_items = total_items + item_in[zi].astype(F32)
    item_unit_grad = INV_TEMP * (total_items - queries[x].astype(F32))
    item_unit, item_scale = unit_rows(item_ref[...])
    item_grad_ref[...] = unit_backward(item_unit_grad, item_unit, item_scale)

    for step in range(1, nz):
        item_copy(step, z).wait_send()
        item_sum_copy(step, z).wait_send()
    for step in range(1, nx):
        query_copy(step, x).wait_send()
        total_copy(step, x).wait_send()
        query_sum_copy(step, x).wait_send()


def local(grid, nx, nz, id_table, w_first, w_second, owner_ids, row_ids):
    pairs, bags = owner_ids.shape
    width, hidden = w_first.shape
    chunk = min(hidden, 512)
    vmem = pl.BlockSpec(memory_space=pltpu.VMEM)
    hbm = pl.BlockSpec(memory_space=pltpu.HBM)
    most = max(nx, nz)
    loss, item_grad, query_grad = pl.pallas_call(
        functools.partial(kernel, grid, nx, nz),
        out_shape=(
            jax.ShapeDtypeStruct((1, pairs), F32),
            jax.ShapeDtypeStruct((pairs, width), F32),
            jax.ShapeDtypeStruct((pairs, width), F32),
        ),
        in_specs=[vmem, hbm, hbm, hbm],
        out_specs=(vmem, vmem, vmem),
        scratch_shapes=[
            pltpu.VMEM((pairs, width), BF16),
            pltpu.VMEM((pairs, width), F32),
            pltpu.VMEM(w_first.shape, BF16),
            pltpu.VMEM(w_second.shape, BF16),
            pltpu.VMEM((hidden // chunk, pairs, chunk), F32),
            pltpu.VMEM((nz, pairs, width), BF16),
            pltpu.VMEM((nx, pairs, width), BF16),
            pltpu.VMEM((nx, nz, pairs, pairs), F32),
            pltpu.VMEM((nx, 1, pairs), F32),
            pltpu.VMEM((nx, nx, 1, pairs), F32),
            pltpu.VMEM((nx, pairs, width), BF16),
            pltpu.VMEM((nx, pairs, width), BF16),
            pltpu.VMEM((nx, nz, pairs, pairs), BF16),
            pltpu.VMEM((pairs, width), F32),
            pltpu.VMEM((nz, pairs, width), BF16),
            pltpu.VMEM((nz, pairs, width), BF16),
            pltpu.VMEM((pairs, width), F32),
            pltpu.SemaphoreType.DMA((2,)),
            pltpu.SemaphoreType.DMA((5, most)),
            pltpu.SemaphoreType.DMA((5, most)),
            *lookup_scratch(grid, bags, pairs, id_table),
        ],
        compiler_params=pltpu.CompilerParams(
            collective_id=0, has_side_effects=True, vmem_limit_bytes=52 * 2**20
        ),
        name="step",
    )((owner_ids * id_table.shape[0] + row_ids).T, id_table, w_first, w_second)
    return loss.reshape(-1), item_grad, query_grad


def solution(mesh):
    blocks, shards = mesh.shape["blk"], mesh.shape["table"]
    nx = math.isqrt(blocks)
    nz = blocks // nx
    grid = (shards // 6, 3, 2)
    placed = (P("table", None), P(), P(), P(("blk", "table"), None), P(("blk", "table"), None))
    return jax.shard_map(
        functools.partial(local, grid, nx, nz),
        mesh=mesh,
        in_specs=placed,
        out_specs=(P(("blk", "table")), P(("blk", "table"), None), P(("blk", "table"), None)),
        check_vma=False,
    )
```

```python
import functools
import math

import jax
import jax.numpy as jnp
from jax import lax
from jax.experimental import pallas as pl
from jax.experimental.pallas import tpu as pltpu
from jax.sharding import PartitionSpec as P

EPS = 1e-06
INV_TEMP = 20.0
MESH = pl.DeviceIdType.MESH
F32 = jnp.float32
BF16 = jnp.bfloat16


def row_dot(left, right):
    return lax.dot_general(left, right, (((1,), (1,)), ((), ())), preferred_element_type=F32)


def col_dot(left, right):
    return lax.dot_general(left, right, (((0,), (0,)), ((), ())), preferred_element_type=F32)


def dot(left, right):
    return jnp.dot(left, right, preferred_element_type=F32)


def unit_rows(vectors):
    scale = lax.rsqrt(jnp.sum(vectors * vectors, axis=-1, keepdims=True) + EPS)
    return vectors * scale, scale


def unit_backward(grad, unit, scale):
    return scale * (grad - unit * jnp.sum(unit * grad, axis=-1, keepdims=True))


def lookup(grid, meet, load, packed_ref, table_ref, refs):
    ny, planes, cores = grid
    (table_bf, table_wide, ids, code_rows, codes, req_all, req_out, req_in, req_smem, rows_out, rows_in, select,
     stage, part_out, part_in, local_sem, ids_send, ids_recv, req_send, req_recv, rows_send, rows_recv,
     part_send, part_recv, smem_sem) = refs
    bags, pairs = packed_ref.shape
    shard_rows, width = table_ref.shape
    cap, half_width = rows_in.shape[3:]
    chunks, chunk = select.shape[1], select.shape[3]
    step_rows = stage.shape[0]
    half = bags // 2
    m = ny * cores
    n = m * planes
    t = lax.axis_index("table")
    plane = (t // cores) % planes
    q = t // (planes * cores) * cores + t % cores

    def shard(place, where):
        return place // cores * (planes * cores) + where * cores + place % cores

    def column(r):
        return {"table": shard(q, lax.rem(plane + r, planes))}

    def across(place):
        return {"table": shard(place, plane)}

    def around(step):
        away = m // 2 - (step + 1) // 2
        return lax.rem(q + away + (step % 2) * (m - 2 * away), m)

    def asker(place, r):
        return shard(place, lax.rem(plane + r, planes))

    pieces = 8
    piece_rows = shard_rows // pieces

    def fetch(piece):
        at = pl.ds(piece * piece_rows, piece_rows)
        return pltpu.make_async_copy(table_ref.at[at, :], table_bf.at[at, :], local_sem.at[piece])

    for piece in range(pieces):
        fetch(piece).start()
    barrier = pltpu.get_barrier_semaphore()

    def greet(step, _):
        other = lax.rem(t + step, n)
        pl.semaphore_signal(barrier, inc=1, device_id={"table": other}, device_id_type=MESH)
        return 0

    lax.fori_loop(1, n, greet, 0)
    others = meet(barrier)

    shard_iota = lax.broadcasted_iota(jnp.int32, (n, pairs), 0)
    shard_place = shard_iota // (planes * cores) * cores + shard_iota % cores
    first_slot = ((shard_iota // cores % planes * m + shard_place) * cap).astype(F32)
    digit_iota = lax.broadcasted_iota(jnp.int32, (2 * cap, pairs), 0)
    low_digit = digit_iota >= cap
    digit_slot = jnp.where(low_digit, digit_iota - cap, digit_iota).astype(F32)
    earlier = jnp.where(
        lax.broadcasted_iota(jnp.int32, (pairs, pairs), 0)
        < lax.broadcasted_iota(jnp.int32, (pairs, pairs), 1),
        1.0, 0.0,
    ).astype(BF16)
    bits = shard_rows.bit_length() - 1
    count = jnp.zeros((n, 1), F32)
    wanted = jnp.zeros((n, 2 * cap), F32)
    for k in range(bags):
        packed = packed_ref[k : k + 1, :]
        hot = jnp.where(packed >> bits == shard_iota, 1.0, 0.0)
        hot_bf = hot.astype(BF16)
        held = dot(hot_bf, earlier) + count
        slot = jnp.sum(hot * held, axis=0, keepdims=True)
        code = slot + jnp.sum(hot * first_slot, axis=0, keepdims=True)
        ids[0, k : k + 1, :] = code.astype(jnp.int32)
        digit = jnp.where(low_digit, packed & 127, (packed & (shard_rows - 1)) >> 7).astype(F32)
        digit = jnp.where(digit_slot == slot, digit, 0.0).astype(BF16)
        wanted = wanted + row_dot(hot_bf, digit)
        count = count + jnp.sum(hot, axis=1, keepdims=True)
    req_all[...] = (wanted * 128.0 + pltpu.roll(wanted, cap, 1)).astype(jnp.int32)

    def split(place, _):
        req_out[place] = req_all[pl.ds(place, 1), :]
        return 0

    lax.fori_loop(0, n, split, 0)
    pl.semaphore_wait(barrier, n - 1 + others)

    def request(place, r, slot, slot_r):
        to = asker(place, r)
        return pltpu.make_async_remote_copy(
            src_ref=req_out.at[to], dst_ref=req_in.at[slot, slot_r],
            send_sem=req_send.at[place, r], recv_sem=req_recv.at[slot, slot_r],
            device_id={"table": to}, device_id_type=MESH,
        )

    def ask(step, _):
        for r in (*range(1, planes), 0):
            request(around(step), r, q, (planes - r) % planes).start()
        return 0

    lax.fori_loop(0, m - 1, ask, 0)
    for r in range(1, planes):
        request(q, r, q, planes - r).start()
    req_in[q, 0] = req_out[t]

    def ids_copy(r, slot):
        return pltpu.make_async_remote_copy(
            src_ref=ids.at[0], dst_ref=ids.at[slot], send_sem=ids_send.at[r], recv_sem=ids_recv.at[slot],
            device_id=column(r), device_id_type=MESH,
        )

    for r in range(1, planes):
        ids_copy(r, planes - r).start()

    blocks = 4
    block_rows = piece_rows // blocks
    for piece in range(pieces):
        fetch(piece).wait()

        def widen(block, _):
            at = pl.ds(pl.multiple_of(piece * piece_rows + block * block_rows, block_rows), block_rows)
            table_wide[at, :] = table_bf[at, :].astype(F32)
            return 0

        lax.fori_loop(0, blocks, widen, 0)
    load()

    def to_smem(place):
        return pltpu.make_async_copy(req_in.at[place], req_smem.at[place], smem_sem.at[place])

    def asked(place):
        for r in range(planes):
            request(place, r, place, r).wait()
        to_smem(place).start()

    def gather(place, r, left, right):
        def some(part, _):
            for s in range(step_rows):
                index = req_smem[place, r, 0, part * step_rows + s] & (shard_rows - 1)
                stage[s : s + 1, :] = table_wide[pl.ds(index, 1), :]
            at = pl.ds(pl.multiple_of(part * step_rows, step_rows), step_rows)
            rows = stage[...].astype(BF16)
            left[at, :] = rows[:, :half_width]
            right[at, :] = rows[:, half_width:]
            return 0

        lax.fori_loop(0, cap // step_rows, some, 0)

    foreign = pl.ds(1, planes - 1)

    def foreign_copy(side, place, slot):
        return pltpu.make_async_remote_copy(
            src_ref=rows_out.at[side, place, foreign], dst_ref=rows_in.at[side, foreign, slot],
            send_sem=rows_send.at[side, place], recv_sem=rows_recv.at[side, slot],
            device_id=across(place), device_id_type=MESH,
        )

    def near_copy(place, slot):
        return pltpu.make_async_remote_copy(
            src_ref=rows_out.at[:, place, 0], dst_ref=rows_in.at[:, 0, slot],
            send_sem=rows_send.at[2, place], recv_sem=rows_recv.at[2, slot],
            device_id=across(place), device_id_type=MESH,
        )

    def serve_foreign(step, _):
        place = around(step)

        @pl.when(step < m - 2)
        def _():
            asked(around(step + 1))

        to_smem(place).wait()
        for r in range(1, planes):
            gather(place, r, rows_out.at[0, place, r], rows_out.at[1, place, r])
        foreign_copy(0, place, q).start()
        return 0

    def serve_second(step, _):
        foreign_copy(1, around(step), q).start()
        return 0

    def collect_near(step, _):
        place = around(step)
        gather(place, 0, rows_out.at[0, place, 0], rows_out.at[1, place, 0])
        return 0

    def serve_near(step, _):
        near_copy(around(step), q).start()
        return 0

    asked(around(0))
    lax.fori_loop(0, m - 1, serve_foreign, 0)
    lax.fori_loop(0, m - 1, serve_second, 0)
    for r in range(1, planes):
        request(q, r, q, r).wait()
    to_smem(q).start()
    to_smem(q).wait()
    for r in range(planes):
        gather(q, r, rows_in.at[0, r, q], rows_in.at[1, r, q])

    code_rows[...] = jnp.zeros_like(code_rows)

    def choose(r):
        code_rows[0:bags, :] = ids[r].astype(F32)
        codes[...] = jnp.transpose(code_rows[...]).astype(jnp.int32) - plane * (m * cap)

        def some(block, _):
            place = lax.broadcasted_iota(jnp.int32, (pairs, chunk), 1) + block * chunk
            for side in range(2):
                mask = codes[:, side * half : side * half + 1] == place
                for k in range(side * half + 1, (side + 1) * half):
                    mask = mask | (codes[:, k : k + 1] == place)
                select[r, block, side * pairs : (side + 1) * pairs, :] = jnp.where(mask, 1.0, 0.0).astype(BF16)
            return 0

        lax.fori_loop(0, chunks, some, 0)

    for r in range(1, planes):
        ids_copy(r, r).wait()
        choose(r)

    def bag_sums(side, r, bag):
        rows = rows_in[side, r].reshape(m * cap, half_width)
        at = slice(bag * pairs, (bag + 1) * pairs)
        total = dot(select[r, 0, at, :], rows[:chunk])
        for block in range(1, chunks):
            total = total + dot(select[r, block, at, :], rows[block * chunk : (block + 1) * chunk])
        return total

    def part_copy(side, r, bag, slot):
        return pltpu.make_async_remote_copy(
            src_ref=part_out.at[side, r, bag], dst_ref=part_in.at[side, slot, bag],
            send_sem=part_send.at[side, r, bag], recv_sem=part_recv.at[side, slot, bag],
            device_id=column(r), device_id_type=MESH,
        )

    for side in range(2):
        def foreign_here(step, _):
            place = around(step)
            foreign_copy(side, place, place).wait()
            return 0

        if side == 1:
            lax.fori_loop(0, m - 1, collect_near, 0)
            lax.fori_loop(0, 2 * m // 3, foreign_here, 0)
            lax.fori_loop(0, m - 1, serve_near, 0)
            lax.fori_loop(2 * m // 3, m - 1, foreign_here, 0)
        else:
            lax.fori_loop(0, m - 1, foreign_here, 0)
        for bag in (1, 0):
            for r in range(1, planes):
                part_out[side, r, bag] = bag_sums(side, r, bag).astype(BF16)
                part_copy(side, r, bag, planes - r).start()

    choose(0)

    def near_here(step, _):
        place = around(step)
        near_copy(place, place).wait()
        return 0

    lax.fori_loop(0, m - 1, near_here, 0)

    def finish(bag, target):
        for side in range(2):
            total = bag_sums(side, 0, bag)
            for r in range(1, planes):
                part_copy(side, r, bag, r).wait()
                total = total + part_in[side, r, bag].astype(F32)
            target[:, side * half_width : (side + 1) * half_width] = total.astype(target.dtype)

    return finish


def lookup_scratch(grid, bags, pairs, table):
    ny, planes, cores = grid
    shard_rows, width = table.shape
    m = ny * cores
    cap = min(pairs, 3 * pairs * bags // (2 * m * planes))
    chunk = min(m * cap, 512)
    dma = pltpu.SemaphoreType.DMA
    return [
        pltpu.VMEM(table.shape, BF16),
        pltpu.VMEM(table.shape, F32),
        pltpu.VMEM((planes, bags, pairs), jnp.int32),
        pltpu.VMEM((128, pairs), F32),
        pltpu.VMEM((pairs, 128), jnp.int32),
        pltpu.VMEM((m * planes, 2 * cap), jnp.int32),
        pltpu.VMEM((m * planes, 1, 2 * cap), jnp.int32),
        pltpu.VMEM((m, planes, 1, 2 * cap), jnp.int32),
        pltpu.SMEM((m, planes, 1, 2 * cap), jnp.int32),
        pltpu.VMEM((2, m, planes, cap, width // 2), BF16),
        pltpu.VMEM((2, planes, m, cap, width // 2), BF16),
        pltpu.VMEM((planes, m * cap // chunk, 2 * pairs, chunk), BF16),
        pltpu.VMEM((16, width), F32),
        pltpu.VMEM((2, planes, 2, pairs, width // 2), BF16),
        pltpu.VMEM((2, planes, 2, pairs, width // 2), BF16),
        dma((8,)),
        dma((planes,)),
        dma((planes,)),
        dma((m, planes)),
        dma((m, planes)),
        dma((3, m)),
        dma((3, m)),
        dma((2, planes, 2)),
        dma((2, planes, 2)),
        dma((m,)),
    ]


def kernel(
    grid, nx, nz, packed_ref, table_hbm, first_hbm, second_hbm, loss_ref, item_grad_ref, query_grad_ref,
    query_ref, item_ref, first, second, slope, items, queries, exps, total_out, total_in,
    query_out, query_in, probs, item_sum, item_out, item_in, acc,
    local_sem, send_sem, recv_sem, *lookup_refs,
):
    blk = lax.axis_index("blk")
    x, z = blk // nz, blk % nz
    pairs, width = query_ref.shape
    steps, chunk = slope.shape[0], slope.shape[2]

    load_first = pltpu.make_async_copy(first_hbm, first, local_sem.at[0])
    load_second = pltpu.make_async_copy(second_hbm, second, local_sem.at[1])

    def load():
        load_first.start()
        load_second.start()

    def along_x(step):
        there = lax.rem(x + step, nx)
        return there, there * nz + z

    def along_z(step):
        there = lax.rem(z + step, nz)
        return there, x * nz + there

    def meet(barrier):
        for axis, count in ((along_x, nx), (along_z, nz)):
            for step in range(1, count):
                pl.semaphore_signal(
                    barrier, inc=1, device_id={"blk": axis(step)[1]}, device_id_type=MESH
                )
        return nx + nz - 2

    finish = lookup(grid, meet, load, packed_ref, table_hbm, lookup_refs)
    finish(1, item_ref)
    item_unit, item_scale = unit_rows(item_ref[...])
    items[z] = item_unit.astype(BF16)

    def copy(phase, source, target, landing, step, axis):
        there, device = axis(step)
        return pltpu.make_async_remote_copy(
            src_ref=source, dst_ref=target,
            send_sem=send_sem.at[phase, there], recv_sem=recv_sem.at[phase, landing],
            device_id={"blk": device}, device_id_type=MESH,
        )

    def item_copy(step, slot):
        return copy(0, items.at[z], items.at[slot], slot, step, along_z)

    def query_copy(step, slot):
        return copy(1, queries.at[x], queries.at[slot], slot, step, along_x)

    def total_copy(step, slot):
        return copy(2, total_out, total_in.at[slot], slot, step, along_x)

    def query_sum_copy(step, slot):
        there = along_x(step)[0]
        return copy(3, query_out.at[there], query_in.at[slot], slot, step, along_x)

    def item_sum_copy(step, slot):
        there = along_z(step)[0]
        return copy(4, item_out.at[there], item_in.at[slot], slot, step, along_z)

    for step in range(1, nz):
        item_copy(step, z).start()

    finish(0, query_ref)
    acc[...] = jnp.zeros_like(acc)
    load_first.wait()
    load_second.wait()

    def forward(part, _):
        at = pl.ds(pl.multiple_of(part * chunk, chunk), chunk)
        pre = dot(query_ref[...], first[:, at])
        sigma = 0.5 + 0.5 * jnp.tanh(0.5 * pre)
        slope[part] = sigma * (1.0 + pre * (1.0 - sigma))
        acc[...] += dot((pre * sigma).astype(BF16), second[at, :])
        return 0

    lax.fori_loop(0, steps, forward, 0)
    query_unit, query_scale = unit_rows(acc[...])
    queries[x] = query_unit.astype(BF16)
    for step in range(1, nx):
        query_copy(step, x).start()

    diagonal = lax.broadcasted_iota(jnp.int32, (pairs, pairs), 0) == lax.broadcasted_iota(
        jnp.int32, (pairs, pairs), 1
    )

    part = jnp.zeros((1, pairs), F32)
    own = None
    for turn in range(nz):
        zi = along_z(turn)[0]
        if turn > 0:
            item_copy(turn, zi).wait_recv()
        scores = INV_TEMP * row_dot(items[zi], queries[x])
        if turn == 0:
            own = jnp.sum(jnp.where(diagonal, scores, 0.0), axis=0, keepdims=True)
        value = jnp.exp(scores)
        exps[0, zi] = value
        part = part + jnp.sum(value, axis=0, keepdims=True)
    total_out[x] = part
    for step in range(1, nx):
        xi = along_x(step)[0]
        query_copy(step, xi).wait_recv()
        value = jnp.exp(INV_TEMP * row_dot(items[...].reshape(nz * pairs, width), queries[xi]))
        exps[step] = value.reshape(nz, pairs, pairs)
        total_out[xi] = jnp.sum(value, axis=0, keepdims=True)
    total_in[x] = total_out[...]
    for step in range(1, nx):
        total_copy(step, x).start()
    for step in range(1, nx):
        total_copy(step, along_x(step)[0]).wait_recv()

    inverse = []
    for step in range(nx):
        xi = along_x(step)[0]
        total = jnp.zeros((1, pairs), F32)
        for source in range(nx):
            total = total + total_in[source, xi]
        if step == 0:
            loss_ref[...] = jnp.log(total) - own
        inverse.append(1.0 / total)

    def item_part(zi):
        part = jnp.zeros((pairs, width), F32)
        for step in range(nx):
            prob = (exps[step, zi] * inverse[step]).astype(BF16)
            probs[step, zi] = prob
            part = part + dot(prob, queries[along_x(step)[0]])
        return part

    def query_part(step):
        return col_dot(probs[step].reshape(nz * pairs, pairs), items[...].reshape(nz * pairs, width))

    for step in range(1, nz):
        zi = along_z(step)[0]
        item_out[zi] = item_part(zi).astype(BF16)
        item_sum_copy(step, z).start()
    item_sum[...] = item_part(z)
    for step in range(1, nx):
        query_out[along_x(step)[0]] = query_part(step).astype(BF16)
        query_sum_copy(step, x).start()
    query_sum = query_part(0)

    for step in range(1, nx):
        xi = along_x(step)[0]
        query_sum_copy(step, xi).wait_recv()
        query_sum = query_sum + query_in[xi].astype(F32)
    query_unit_grad = INV_TEMP * (query_sum - items[z].astype(F32))
    query_unit = acc[...] * query_scale
    out_grad = unit_backward(query_unit_grad, query_unit, query_scale).astype(BF16)
    acc[...] = jnp.zeros_like(acc)

    def backward(part, _):
        at = pl.ds(pl.multiple_of(part * chunk, chunk), chunk)
        hidden_grad = (row_dot(out_grad, second[at, :]) * slope[part]).astype(BF16)
        acc[...] += row_dot(hidden_grad, first[:, at])
        return 0

    lax.fori_loop(0, steps, backward, 0)
    query_grad_ref[...] = acc[...]

    total_items = item_sum[...]
    for step in range(1, nz):
        zi = along_z(step)[0]
        item_sum_copy(step, zi).wait_recv()
        total_items = total_items + item_in[zi].astype(F32)
    item_unit_grad = INV_TEMP * (total_items - queries[x].astype(F32))
    item_unit, item_scale = unit_rows(item_ref[...])
    item_grad_ref[...] = unit_backward(item_unit_grad, item_unit, item_scale)

    for step in range(1, nz):
        item_copy(step, z).wait_send()
        item_sum_copy(step, z).wait_send()
    for step in range(1, nx):
        query_copy(step, x).wait_send()
        total_copy(step, x).wait_send()
        query_sum_copy(step, x).wait_send()


def local(grid, nx, nz, id_table, w_first, w_second, owner_ids, row_ids):
    pairs, bags = owner_ids.shape
    width, hidden = w_first.shape
    chunk = min(hidden, 512)
    vmem = pl.BlockSpec(memory_space=pltpu.VMEM)
    hbm = pl.BlockSpec(memory_space=pltpu.HBM)
    most = max(nx, nz)
    loss, item_grad, query_grad = pl.pallas_call(
        functools.partial(kernel, grid, nx, nz),
        out_shape=(
            jax.ShapeDtypeStruct((1, pairs), F32),
            jax.ShapeDtypeStruct((pairs, width), F32),
            jax.ShapeDtypeStruct((pairs, width), F32),
        ),
        in_specs=[vmem, hbm, hbm, hbm],
        out_specs=(vmem, vmem, vmem),
        scratch_shapes=[
            pltpu.VMEM((pairs, width), BF16),
            pltpu.VMEM((pairs, width), F32),
            pltpu.VMEM(w_first.shape, BF16),
            pltpu.VMEM(w_second.shape, BF16),
            pltpu.VMEM((hidden // chunk, pairs, chunk), F32),
            pltpu.VMEM((nz, pairs, width), BF16),
            pltpu.VMEM((nx, pairs, width), BF16),
            pltpu.VMEM((nx, nz, pairs, pairs), F32),
            pltpu.VMEM((nx, 1, pairs), F32),
            pltpu.VMEM((nx, nx, 1, pairs), F32),
            pltpu.VMEM((nx, pairs, width), BF16),
            pltpu.VMEM((nx, pairs, width), BF16),
            pltpu.VMEM((nx, nz, pairs, pairs), BF16),
            pltpu.VMEM((pairs, width), F32),
            pltpu.VMEM((nz, pairs, width), BF16),
            pltpu.VMEM((nz, pairs, width), BF16),
            pltpu.VMEM((pairs, width), F32),
            pltpu.SemaphoreType.DMA((2,)),
            pltpu.SemaphoreType.DMA((5, most)),
            pltpu.SemaphoreType.DMA((5, most)),
            *lookup_scratch(grid, bags, pairs, id_table),
        ],
        compiler_params=pltpu.CompilerParams(
            collective_id=0, has_side_effects=True, vmem_limit_bytes=52 * 2**20
        ),
        name="step",
    )((owner_ids * id_table.shape[0] + row_ids).T, id_table, w_first, w_second)
    return loss.reshape(-1), item_grad, query_grad


def solution(mesh):
    blocks, shards = mesh.shape["blk"], mesh.shape["table"]
    nx = math.isqrt(blocks)
    nz = blocks // nx
    grid = (shards // 6, 3, 2)
    placed = (P("table", None), P(), P(), P(("blk", "table"), None), P(("blk", "table"), None))
    return jax.shard_map(
        functools.partial(local, grid, nx, nz),
        mesh=mesh,
        in_specs=placed,
        out_specs=(P(("blk", "table")), P(("blk", "table"), None), P(("blk", "table"), None)),
        check_vma=False,
    )
```

```python
import functools
import math

import jax
import jax.numpy as jnp
from jax import lax
from jax.experimental import pallas as pl
from jax.experimental.pallas import tpu as pltpu
from jax.sharding import PartitionSpec as P

EPS = 1e-06
INV_TEMP = 20.0
MESH = pl.DeviceIdType.MESH
F32 = jnp.float32
BF16 = jnp.bfloat16


def row_dot(left, right):
    return lax.dot_general(left, right, (((1,), (1,)), ((), ())), preferred_element_type=F32)


def col_dot(left, right):
    return lax.dot_general(left, right, (((0,), (0,)), ((), ())), preferred_element_type=F32)


def dot(left, right):
    return jnp.dot(left, right, preferred_element_type=F32)


def unit_rows(vectors):
    scale = lax.rsqrt(jnp.sum(vectors * vectors, axis=-1, keepdims=True) + EPS)
    return vectors * scale, scale


def unit_backward(grad, unit, scale):
    return scale * (grad - unit * jnp.sum(unit * grad, axis=-1, keepdims=True))


def lookup(grid, meet, load, packed_ref, table_ref, refs):
    ny, planes, cores = grid
    (table_bf, table_wide, ids, code_rows, codes, req_all, req_out, req_in, req_smem, rows_out, rows_in, select,
     stage, part_out, part_in, local_sem, ids_send, ids_recv, req_send, req_recv, rows_send, rows_recv,
     part_send, part_recv, smem_sem) = refs
    bags, pairs = packed_ref.shape
    shard_rows, width = table_ref.shape
    cap, half_width = rows_in.shape[3:]
    chunks, chunk = select.shape[1], select.shape[3]
    step_rows = stage.shape[0]
    half = bags // 2
    m = ny * cores
    n = m * planes
    t = lax.axis_index("table")
    plane = (t // cores) % planes
    q = t // (planes * cores) * cores + t % cores

    def shard(place, where):
        return place // cores * (planes * cores) + where * cores + place % cores

    def column(r):
        return {"table": shard(q, lax.rem(plane + r, planes))}

    def across(place):
        return {"table": shard(place, plane)}

    def around(step):
        away = m // 2 - (step + 1) // 2
        return lax.rem(q + away + (step % 2) * (m - 2 * away), m)

    def asker(place, r):
        return shard(place, lax.rem(plane + r, planes))

    pieces = 8
    piece_rows = shard_rows // pieces

    def fetch(piece):
        at = pl.ds(piece * piece_rows, piece_rows)
        return pltpu.make_async_copy(table_ref.at[at, :], table_bf.at[at, :], local_sem.at[piece])

    for piece in range(pieces):
        fetch(piece).start()
    barrier = pltpu.get_barrier_semaphore()

    def greet(step, _):
        other = lax.rem(t + step, n)
        pl.semaphore_signal(barrier, inc=1, device_id={"table": other}, device_id_type=MESH)
        return 0

    lax.fori_loop(1, n, greet, 0)
    others = meet(barrier)

    shard_iota = lax.broadcasted_iota(jnp.int32, (n, pairs), 0)
    shard_place = shard_iota // (planes * cores) * cores + shard_iota % cores
    first_slot = ((shard_iota // cores % planes * m + shard_place) * cap).astype(F32)
    digit_iota = lax.broadcasted_iota(jnp.int32, (2 * cap, pairs), 0)
    low_digit = digit_iota >= cap
    digit_slot = jnp.where(low_digit, digit_iota - cap, digit_iota).astype(F32)
    earlier = jnp.where(
        lax.broadcasted_iota(jnp.int32, (pairs, pairs), 0)
        < lax.broadcasted_iota(jnp.int32, (pairs, pairs), 1),
        1.0, 0.0,
    ).astype(BF16)
    bits = shard_rows.bit_length() - 1
    count = jnp.zeros((n, 1), F32)
    wanted = jnp.zeros((n, 2 * cap), F32)
    for k in range(bags):
        packed = packed_ref[k : k + 1, :]
        hot = jnp.where(packed >> bits == shard_iota, 1.0, 0.0)
        hot_bf = hot.astype(BF16)
        held = dot(hot_bf, earlier) + count
        slot = jnp.sum(hot * held, axis=0, keepdims=True)
        code = slot + jnp.sum(hot * first_slot, axis=0, keepdims=True)
        ids[0, k : k + 1, :] = code.astype(jnp.int32)
        digit = jnp.where(low_digit, packed & 127, (packed & (shard_rows - 1)) >> 7).astype(F32)
        digit = jnp.where(digit_slot == slot, digit, 0.0).astype(BF16)
        wanted = wanted + row_dot(hot_bf, digit)
        count = count + jnp.sum(hot, axis=1, keepdims=True)
    req_all[...] = (wanted * 128.0 + pltpu.roll(wanted, cap, 1)).astype(jnp.int32)

    def split(place, _):
        req_out[place] = req_all[pl.ds(place, 1), :]
        return 0

    lax.fori_loop(0, n, split, 0)
    pl.semaphore_wait(barrier, n - 1 + others)

    def request(place, r, slot, slot_r):
        to = asker(place, r)
        return pltpu.make_async_remote_copy(
            src_ref=req_out.at[to], dst_ref=req_in.at[slot, slot_r],
            send_sem=req_send.at[place, r], recv_sem=req_recv.at[slot, slot_r],
            device_id={"table": to}, device_id_type=MESH,
        )

    def ask(step, _):
        for r in (*range(1, planes), 0):
            request(around(step), r, q, (planes - r) % planes).start()
        return 0

    lax.fori_loop(0, m - 1, ask, 0)
    for r in range(1, planes):
        request(q, r, q, planes - r).start()
    req_in[q, 0] = req_out[t]

    def ids_copy(r, slot):
        return pltpu.make_async_remote_copy(
            src_ref=ids.at[0], dst_ref=ids.at[slot], send_sem=ids_send.at[r], recv_sem=ids_recv.at[slot],
            device_id=column(r), device_id_type=MESH,
        )

    for r in range(1, planes):
        ids_copy(r, planes - r).start()

    blocks = 4
    block_rows = piece_rows // blocks
    for piece in range(pieces):
        fetch(piece).wait()

        def widen(block, _):
            at = pl.ds(pl.multiple_of(piece * piece_rows + block * block_rows, block_rows), block_rows)
            table_wide[at, :] = table_bf[at, :].astype(F32)
            return 0

        lax.fori_loop(0, blocks, widen, 0)
    load()

    def to_smem(place):
        return pltpu.make_async_copy(req_in.at[place], req_smem.at[place], smem_sem.at[place])

    def asked(place):
        for r in range(planes):
            request(place, r, place, r).wait()
        to_smem(place).start()

    def gather(place, r, left, right):
        def some(part, _):
            for s in range(step_rows):
                index = req_smem[place, r, 0, part * step_rows + s] & (shard_rows - 1)
                stage[s : s + 1, :] = table_wide[pl.ds(index, 1), :]
            at = pl.ds(pl.multiple_of(part * step_rows, step_rows), step_rows)
            rows = stage[...].astype(BF16)
            left[at, :] = rows[:, :half_width]
            right[at, :] = rows[:, half_width:]
            return 0

        lax.fori_loop(0, cap // step_rows, some, 0)

    foreign = pl.ds(1, planes - 1)

    def foreign_copy(side, place, slot):
        return pltpu.make_async_remote_copy(
            src_ref=rows_out.at[side, place, foreign], dst_ref=rows_in.at[side, foreign, slot],
            send_sem=rows_send.at[side, place], recv_sem=rows_recv.at[side, slot],
            device_id=across(place), device_id_type=MESH,
        )

    def near_copy(place, slot):
        return pltpu.make_async_remote_copy(
            src_ref=rows_out.at[:, place, 0], dst_ref=rows_in.at[:, 0, slot],
            send_sem=rows_send.at[2, place], recv_sem=rows_recv.at[2, slot],
            device_id=across(place), device_id_type=MESH,
        )

    def serve_foreign(step, _):
        place = around(step)

        @pl.when(step < m - 2)
        def _():
            asked(around(step + 1))

        to_smem(place).wait()
        for r in range(1, planes):
            gather(place, r, rows_out.at[0, place, r], rows_out.at[1, place, r])
        foreign_copy(0, place, q).start()
        return 0

    def serve_second(step, _):
        foreign_copy(1, around(step), q).start()
        return 0

    def collect_near(step, _):
        place = around(step)
        gather(place, 0, rows_out.at[0, place, 0], rows_out.at[1, place, 0])
        return 0

    def serve_near(step, _):
        near_copy(around(step), q).start()
        return 0

    asked(around(0))
    lax.fori_loop(0, m - 1, serve_foreign, 0)
    lax.fori_loop(0, m - 1, serve_second, 0)
    for r in range(1, planes):
        request(q, r, q, r).wait()
    to_smem(q).start()
    to_smem(q).wait()
    for r in range(planes):
        gather(q, r, rows_in.at[0, r, q], rows_in.at[1, r, q])

    code_rows[...] = jnp.zeros_like(code_rows)

    def choose(r):
        code_rows[0:bags, :] = ids[r].astype(F32)
        codes[...] = jnp.transpose(code_rows[...]).astype(jnp.int32) - plane * (m * cap)

        def some(block, _):
            place = lax.broadcasted_iota(jnp.int32, (pairs, chunk), 1) + block * chunk
            for side in range(2):
                mask = codes[:, side * half : side * half + 1] == place
                for k in range(side * half + 1, (side + 1) * half):
                    mask = mask | (codes[:, k : k + 1] == place)
                select[r, block, side * pairs : (side + 1) * pairs, :] = jnp.where(mask, 1.0, 0.0).astype(BF16)
            return 0

        lax.fori_loop(0, chunks, some, 0)

    for r in range(1, planes):
        ids_copy(r, r).wait()
        choose(r)

    def bag_sums(side, r, bag):
        rows = rows_in[side, r].reshape(m * cap, half_width)
        at = slice(bag * pairs, (bag + 1) * pairs)
        total = dot(select[r, 0, at, :], rows[:chunk])
        for block in range(1, chunks):
            total = total + dot(select[r, block, at, :], rows[block * chunk : (block + 1) * chunk])
        return total

    def part_copy(side, r, bag, slot):
        return pltpu.make_async_remote_copy(
            src_ref=part_out.at[side, r, bag], dst_ref=part_in.at[side, slot, bag],
            send_sem=part_send.at[side, r, bag], recv_sem=part_recv.at[side, slot, bag],
            device_id=column(r), device_id_type=MESH,
        )

    for side in range(2):
        def foreign_here(step, _):
            place = around(step)
            foreign_copy(side, place, place).wait()
            return 0

        if side == 1:
            lax.fori_loop(0, m - 1, collect_near, 0)
            lax.fori_loop(0, 2 * m // 3, foreign_here, 0)
            lax.fori_loop(0, m - 1, serve_near, 0)
            lax.fori_loop(2 * m // 3, m - 1, foreign_here, 0)
        else:
            lax.fori_loop(0, m - 1, foreign_here, 0)
        for bag in (1, 0):
            for r in range(1, planes):
                part_out[side, r, bag] = bag_sums(side, r, bag).astype(BF16)
                part_copy(side, r, bag, planes - r).start()

    choose(0)

    def near_here(step, _):
        place = around(step)
        near_copy(place, place).wait()
        return 0

    lax.fori_loop(0, m - 1, near_here, 0)

    def finish(bag, target):
        for side in range(2):
            total = bag_sums(side, 0, bag)
            for r in range(1, planes):
                part_copy(side, r, bag, r).wait()
                total = total + part_in[side, r, bag].astype(F32)
            target[:, side * half_width : (side + 1) * half_width] = total.astype(target.dtype)

    return finish


def lookup_scratch(grid, bags, pairs, table):
    ny, planes, cores = grid
    shard_rows, width = table.shape
    m = ny * cores
    cap = min(pairs, 3 * pairs * bags // (2 * m * planes))
    chunk = min(m * cap, 512)
    dma = pltpu.SemaphoreType.DMA
    return [
        pltpu.VMEM(table.shape, BF16),
        pltpu.VMEM(table.shape, F32),
        pltpu.VMEM((planes, bags, pairs), jnp.int32),
        pltpu.VMEM((128, pairs), F32),
        pltpu.VMEM((pairs, 128), jnp.int32),
        pltpu.VMEM((m * planes, 2 * cap), jnp.int32),
        pltpu.VMEM((m * planes, 1, 2 * cap), jnp.int32),
        pltpu.VMEM((m, planes, 1, 2 * cap), jnp.int32),
        pltpu.SMEM((m, planes, 1, 2 * cap), jnp.int32),
        pltpu.VMEM((2, m, planes, cap, width // 2), BF16),
        pltpu.VMEM((2, planes, m, cap, width // 2), BF16),
        pltpu.VMEM((planes, m * cap // chunk, 2 * pairs, chunk), BF16),
        pltpu.VMEM((16, width), F32),
        pltpu.VMEM((2, planes, 2, pairs, width // 2), BF16),
        pltpu.VMEM((2, planes, 2, pairs, width // 2), BF16),
        dma((8,)),
        dma((planes,)),
        dma((planes,)),
        dma((m, planes)),
        dma((m, planes)),
        dma((3, m)),
        dma((3, m)),
        dma((2, planes, 2)),
        dma((2, planes, 2)),
        dma((m,)),
    ]


def kernel(
    grid, nx, nz, packed_ref, table_hbm, first_hbm, second_hbm, loss_ref, item_grad_ref, query_grad_ref,
    query_ref, item_ref, first, second, slope, items, queries, exps, total_out, total_in,
    query_out, query_in, probs, item_sum, item_out, item_in, passed, acc,
    local_sem, send_sem, recv_sem, *lookup_refs,
):
    blk = lax.axis_index("blk")
    x, z = blk // nz, blk % nz
    pairs, width = query_ref.shape
    steps, chunk = slope.shape[0], slope.shape[2]

    load_first = pltpu.make_async_copy(first_hbm, first, local_sem.at[0])
    load_second = pltpu.make_async_copy(second_hbm, second, local_sem.at[1])

    def load():
        load_first.start()
        load_second.start()

    def along_x(step):
        there = lax.rem(x + step, nx)
        return there, there * nz + z

    def along_z(step):
        there = lax.rem(z + step, nz)
        return there, x * nz + there

    def meet(barrier):
        for axis, count in ((along_x, nx), (along_z, nz)):
            for step in range(1, count):
                pl.semaphore_signal(
                    barrier, inc=1, device_id={"blk": axis(step)[1]}, device_id_type=MESH
                )
        return nx + nz - 2

    finish = lookup(grid, meet, load, packed_ref, table_hbm, lookup_refs)
    finish(1, item_ref)
    item_unit, item_scale = unit_rows(item_ref[...])
    items[z] = item_unit.astype(BF16)

    def copy(phase, source, target, landing, step, axis):
        there, device = axis(step)
        return pltpu.make_async_remote_copy(
            src_ref=source, dst_ref=target,
            send_sem=send_sem.at[phase, there], recv_sem=recv_sem.at[phase, landing],
            device_id={"blk": device}, device_id_type=MESH,
        )

    def item_copy(step, slot):
        return copy(0, items.at[z], items.at[slot], slot, step, along_z)

    def query_copy(step, slot):
        return copy(1, queries.at[x], queries.at[slot], slot, step, along_x)

    def total_copy(step, slot):
        return copy(2, total_out, total_in.at[slot], slot, step, along_x)

    def query_sum_copy(step, slot):
        there = along_x(step)[0]
        return copy(3, query_out.at[there], query_in.at[slot], slot, step, along_x)

    def item_sum_copy(step, slot):
        there = along_z(step)[0]
        return copy(4, item_out.at[there], item_in.at[slot], slot, step, along_z)

    middle = (z == 1) | (z == 2)
    end = (z == 0) | (z == 3)
    far = 3 * (2 - z)

    def not_across(step):
        return middle | (z + along_z(step)[0] != 3)

    def item_forward():
        return pltpu.make_async_remote_copy(
            src_ref=items.at[far], dst_ref=items.at[far],
            send_sem=send_sem.at[0, z], recv_sem=recv_sem.at[0, far],
            device_id={"blk": x * nz + 3 - far}, device_id_type=MESH,
        )

    def item_pass():
        between = 1 + z // 3
        return pltpu.make_async_remote_copy(
            src_ref=item_out.at[3 - z], dst_ref=passed,
            send_sem=send_sem.at[5, 0], recv_sem=recv_sem.at[5, 0],
            device_id={"blk": x * nz + between}, device_id_type=MESH,
        )

    for step in (2, 1, 3):
        @pl.when(not_across(step))
        def _():
            item_copy(step, z).start()

    finish(0, query_ref)
    acc[...] = jnp.zeros_like(acc)
    load_first.wait()
    load_second.wait()

    def forward(part, _):
        at = pl.ds(pl.multiple_of(part * chunk, chunk), chunk)
        pre = dot(query_ref[...], first[:, at])
        sigma = 0.5 + 0.5 * jnp.tanh(0.5 * pre)
        slope[part] = sigma * (1.0 + pre * (1.0 - sigma))
        acc[...] += dot((pre * sigma).astype(BF16), second[at, :])
        return 0

    lax.fori_loop(0, steps, forward, 0)
    query_unit, query_scale = unit_rows(acc[...])
    queries[x] = query_unit.astype(BF16)
    for step in range(1, nx):
        query_copy(step, x).start()

    @pl.when(middle)
    def _():
        item_copy(2, far).wait_recv()
        item_forward().start()

    diagonal = lax.broadcasted_iota(jnp.int32, (pairs, pairs), 0) == lax.broadcasted_iota(
        jnp.int32, (pairs, pairs), 1
    )

    part = jnp.zeros((1, pairs), F32)
    own = None
    for turn in range(nz):
        zi = along_z(turn)[0]
        if turn == 2:
            @pl.when(end)
            def _():
                item_copy(turn, zi).wait_recv()
        elif turn > 0:
            item_copy(turn, zi).wait_recv()
        scores = INV_TEMP * row_dot(items[zi], queries[x])
        if turn == 0:
            own = jnp.sum(jnp.where(diagonal, scores, 0.0), axis=0, keepdims=True)
        value = jnp.exp(scores)
        exps[0, zi] = value
        part = part + jnp.sum(value, axis=0, keepdims=True)
    total_out[x] = part
    for step in range(1, nx):
        xi = along_x(step)[0]
        query_copy(step, xi).wait_recv()
        value = jnp.exp(INV_TEMP * row_dot(items[...].reshape(nz * pairs, width), queries[xi]))
        exps[step] = value.reshape(nz, pairs, pairs)
        total_out[xi] = jnp.sum(value, axis=0, keepdims=True)
    total_in[x] = total_out[...]
    for step in range(1, nx):
        total_copy(step, x).start()
    for step in range(1, nx):
        total_copy(step, along_x(step)[0]).wait_recv()

    inverse = []
    for step in range(nx):
        xi = along_x(step)[0]
        total = jnp.zeros((1, pairs), F32)
        for source in range(nx):
            total = total + total_in[source, xi]
        if step == 0:
            loss_ref[...] = jnp.log(total) - own
        inverse.append(1.0 / total)

    def item_part(zi):
        part = jnp.zeros((pairs, width), F32)
        for step in range(nx):
            prob = (exps[step, zi] * inverse[step]).astype(BF16)
            probs[step, zi] = prob
            part = part + dot(prob, queries[along_x(step)[0]])
        return part

    def query_part(step):
        return col_dot(probs[step].reshape(nz * pairs, pairs), items[...].reshape(nz * pairs, width))

    def item_sum_to(there):
        return pltpu.make_async_remote_copy(
            src_ref=item_out.at[there], dst_ref=item_in.at[z],
            send_sem=send_sem.at[4, there], recv_sem=recv_sem.at[4, z],
            device_id={"blk": x * nz + there}, device_id_type=MESH,
        )

    first_to, second_to = 3 - z, (2 + 3 * z) % 5
    third_to = 6 - z - first_to - second_to
    item_out[first_to] = item_part(first_to).astype(BF16)

    @pl.when(middle)
    def _():
        item_sum_to(first_to).start()

    @pl.when(end)
    def _():
        item_pass().start()

    item_out[second_to] = item_part(second_to).astype(BF16)
    item_sum_to(second_to).start()
    item_sum[...] = item_part(third_to)

    @pl.when(end)
    def _():
        item_out[third_to] = item_sum[...].astype(BF16)
        item_sum_to(third_to).start()

    own_part = item_part(z)
    for step in range(1, nx):
        query_out[along_x(step)[0]] = query_part(step).astype(BF16)
        query_sum_copy(step, x).start()
    query_sum = query_part(0)

    @pl.when(middle)
    def _():
        item_pass().wait_recv()
        item_out[third_to] = (item_sum[...] + passed[...].astype(F32)).astype(BF16)
        item_sum_to(third_to).start()

    item_sum[...] = own_part

    for step in range(1, nx):
        xi = along_x(step)[0]
        query_sum_copy(step, xi).wait_recv()
        query_sum = query_sum + query_in[xi].astype(F32)
    query_unit_grad = INV_TEMP * (query_sum - items[z].astype(F32))
    query_unit = acc[...] * query_scale
    out_grad = unit_backward(query_unit_grad, query_unit, query_scale).astype(BF16)
    acc[...] = jnp.zeros_like(acc)

    def backward(part, _):
        at = pl.ds(pl.multiple_of(part * chunk, chunk), chunk)
        hidden_grad = (row_dot(out_grad, second[at, :]) * slope[part]).astype(BF16)
        acc[...] += row_dot(hidden_grad, first[:, at])
        return 0

    lax.fori_loop(0, steps, backward, 0)
    query_grad_ref[...] = acc[...]

    for step in range(1, nz):
        @pl.when(not_across(step))
        def _():
            zi = along_z(step)[0]
            item_sum_copy(step, zi).wait_recv()
            item_sum[...] += item_in[zi].astype(F32)
    total_items = item_sum[...]
    item_unit_grad = INV_TEMP * (total_items - queries[x].astype(F32))
    item_unit, item_scale = unit_rows(item_ref[...])
    item_grad_ref[...] = unit_backward(item_unit_grad, item_unit, item_scale)

    for step in range(1, nz):
        @pl.when(not_across(step))
        def _():
            item_copy(step, z).wait_send()
            item_sum_copy(step, z).wait_send()

    @pl.when(middle)
    def _():
        item_forward().wait_send()

    @pl.when(end)
    def _():
        item_pass().wait_send()

    for step in range(1, nx):
        query_copy(step, x).wait_send()
        total_copy(step, x).wait_send()
        query_sum_copy(step, x).wait_send()


def local(grid, nx, nz, id_table, w_first, w_second, owner_ids, row_ids):
    pairs, bags = owner_ids.shape
    width, hidden = w_first.shape
    chunk = min(hidden, 512)
    vmem = pl.BlockSpec(memory_space=pltpu.VMEM)
    hbm = pl.BlockSpec(memory_space=pltpu.HBM)
    most = max(nx, nz)
    loss, item_grad, query_grad = pl.pallas_call(
        functools.partial(kernel, grid, nx, nz),
        out_shape=(
            jax.ShapeDtypeStruct((1, pairs), F32),
            jax.ShapeDtypeStruct((pairs, width), F32),
            jax.ShapeDtypeStruct((pairs, width), F32),
        ),
        in_specs=[vmem, hbm, hbm, hbm],
        out_specs=(vmem, vmem, vmem),
        scratch_shapes=[
            pltpu.VMEM((pairs, width), BF16),
            pltpu.VMEM((pairs, width), F32),
            pltpu.VMEM(w_first.shape, BF16),
            pltpu.VMEM(w_second.shape, BF16),
            pltpu.VMEM((hidden // chunk, pairs, chunk), F32),
            pltpu.VMEM((nz, pairs, width), BF16),
            pltpu.VMEM((nx, pairs, width), BF16),
            pltpu.VMEM((nx, nz, pairs, pairs), F32),
            pltpu.VMEM((nx, 1, pairs), F32),
            pltpu.VMEM((nx, nx, 1, pairs), F32),
            pltpu.VMEM((nx, pairs, width), BF16),
            pltpu.VMEM((nx, pairs, width), BF16),
            pltpu.VMEM((nx, nz, pairs, pairs), BF16),
            pltpu.VMEM((pairs, width), F32),
            pltpu.VMEM((nz, pairs, width), BF16),
            pltpu.VMEM((nz, pairs, width), BF16),
            pltpu.VMEM((pairs, width), BF16),
            pltpu.VMEM((pairs, width), F32),
            pltpu.SemaphoreType.DMA((2,)),
            pltpu.SemaphoreType.DMA((6, most)),
            pltpu.SemaphoreType.DMA((6, most)),
            *lookup_scratch(grid, bags, pairs, id_table),
        ],
        compiler_params=pltpu.CompilerParams(
            collective_id=0, has_side_effects=True, vmem_limit_bytes=52 * 2**20
        ),
        name="step",
    )((owner_ids * id_table.shape[0] + row_ids).T, id_table, w_first, w_second)
    return loss.reshape(-1), item_grad, query_grad


def solution(mesh):
    blocks, shards = mesh.shape["blk"], mesh.shape["table"]
    nx = math.isqrt(blocks)
    nz = blocks // nx
    grid = (shards // 6, 3, 2)
    placed = (P("table", None), P(), P(), P(("blk", "table"), None), P(("blk", "table"), None))
    return jax.shard_map(
        functools.partial(local, grid, nx, nz),
        mesh=mesh,
        in_specs=placed,
        out_specs=(P(("blk", "table")), P(("blk", "table"), None), P(("blk", "table"), None)),
        check_vma=False,
    )
```

```python
import functools
import math

import jax
import jax.numpy as jnp
from jax import lax
from jax.experimental import pallas as pl
from jax.experimental.pallas import tpu as pltpu
from jax.sharding import PartitionSpec as P

EPS = 1e-06
INV_TEMP = 20.0
MESH = pl.DeviceIdType.MESH
F32 = jnp.float32
BF16 = jnp.bfloat16


def row_dot(left, right):
    return lax.dot_general(left, right, (((1,), (1,)), ((), ())), preferred_element_type=F32)


def col_dot(left, right):
    return lax.dot_general(left, right, (((0,), (0,)), ((), ())), preferred_element_type=F32)


def dot(left, right):
    return jnp.dot(left, right, preferred_element_type=F32)


def unit_rows(vectors):
    scale = lax.rsqrt(jnp.sum(vectors * vectors, axis=-1, keepdims=True) + EPS)
    return vectors * scale, scale


def unit_backward(grad, unit, scale):
    return scale * (grad - unit * jnp.sum(unit * grad, axis=-1, keepdims=True))


def lookup(grid, meet, load, packed_ref, table_ref, refs):
    ny, planes, cores = grid
    (table_bf, table_wide, ids, code_rows, codes, req_all, req_out, req_in, req_smem, rows_out, rows_in, select,
     stage, part_out, part_in, local_sem, ids_send, ids_recv, req_send, req_recv, rows_send, rows_recv,
     part_send, part_recv, smem_sem) = refs
    bags, pairs = packed_ref.shape
    shard_rows, width = table_ref.shape
    cap, half_width = rows_in.shape[3:]
    chunks, chunk = select.shape[1], select.shape[3]
    step_rows = stage.shape[0]
    half = bags // 2
    m = ny * cores
    n = m * planes
    t = lax.axis_index("table")
    plane = (t // cores) % planes
    q = t // (planes * cores) * cores + t % cores

    def shard(place, where):
        return place // cores * (planes * cores) + where * cores + place % cores

    def column(r):
        return {"table": shard(q, lax.rem(plane + r, planes))}

    def across(place):
        return {"table": shard(place, plane)}

    def around(step):
        away = m // 2 - (step + 1) // 2
        return lax.rem(q + away + (step % 2) * (m - 2 * away), m)

    def asker(place, r):
        return shard(place, lax.rem(plane + r, planes))

    pieces = 8
    piece_rows = shard_rows // pieces

    def fetch(piece):
        at = pl.ds(piece * piece_rows, piece_rows)
        return pltpu.make_async_copy(table_ref.at[at, :], table_bf.at[at, :], local_sem.at[piece])

    for piece in range(pieces):
        fetch(piece).start()
    barrier = pltpu.get_barrier_semaphore()

    def greet(step, _):
        other = lax.rem(t + step, n)
        pl.semaphore_signal(barrier, inc=1, device_id={"table": other}, device_id_type=MESH)
        return 0

    lax.fori_loop(1, n, greet, 0)
    others = meet(barrier)

    shard_iota = lax.broadcasted_iota(jnp.int32, (n, pairs), 0)
    shard_place = shard_iota // (planes * cores) * cores + shard_iota % cores
    first_slot = ((shard_iota // cores % planes * m + shard_place) * cap).astype(F32)
    digit_iota = lax.broadcasted_iota(jnp.int32, (2 * cap, pairs), 0)
    low_digit = digit_iota >= cap
    digit_slot = jnp.where(low_digit, digit_iota - cap, digit_iota).astype(F32)
    earlier = jnp.where(
        lax.broadcasted_iota(jnp.int32, (pairs, pairs), 0)
        < lax.broadcasted_iota(jnp.int32, (pairs, pairs), 1),
        1.0, 0.0,
    ).astype(BF16)
    bits = shard_rows.bit_length() - 1
    count = jnp.zeros((n, 1), F32)
    wanted = jnp.zeros((n, 2 * cap), F32)
    for k in range(bags):
        packed = packed_ref[k : k + 1, :]
        hot = jnp.where(packed >> bits == shard_iota, 1.0, 0.0)
        hot_bf = hot.astype(BF16)
        held = dot(hot_bf, earlier) + count
        slot = jnp.sum(hot * held, axis=0, keepdims=True)
        code = slot + jnp.sum(hot * first_slot, axis=0, keepdims=True)
        ids[0, k : k + 1, :] = code.astype(jnp.int32)
        digit = jnp.where(low_digit, packed & 127, (packed & (shard_rows - 1)) >> 7).astype(F32)
        digit = jnp.where(digit_slot == slot, digit, 0.0).astype(BF16)
        wanted = wanted + row_dot(hot_bf, digit)
        count = count + jnp.sum(hot, axis=1, keepdims=True)
    req_all[...] = (wanted * 128.0 + pltpu.roll(wanted, cap, 1)).astype(jnp.int32)

    def split(place, _):
        req_out[place] = req_all[pl.ds(place, 1), :]
        return 0

    lax.fori_loop(0, n, split, 0)
    pl.semaphore_wait(barrier, n - 1 + others)

    def request(place, r, slot, slot_r):
        to = asker(place, r)
        return pltpu.make_async_remote_copy(
            src_ref=req_out.at[to], dst_ref=req_in.at[slot, slot_r],
            send_sem=req_send.at[place, r], recv_sem=req_recv.at[slot, slot_r],
            device_id={"table": to}, device_id_type=MESH,
        )

    def ask(step, _):
        for r in (*range(1, planes), 0):
            request(around(step), r, q, (planes - r) % planes).start()
        return 0

    lax.fori_loop(0, m - 1, ask, 0)
    for r in range(1, planes):
        request(q, r, q, planes - r).start()
    req_in[q, 0] = req_out[t]

    def ids_copy(r, slot):
        return pltpu.make_async_remote_copy(
            src_ref=ids.at[0], dst_ref=ids.at[slot], send_sem=ids_send.at[r], recv_sem=ids_recv.at[slot],
            device_id=column(r), device_id_type=MESH,
        )

    for r in range(1, planes):
        ids_copy(r, planes - r).start()

    blocks = 4
    block_rows = piece_rows // blocks
    for piece in range(pieces):
        fetch(piece).wait()

        def widen(block, _):
            at = pl.ds(pl.multiple_of(piece * piece_rows + block * block_rows, block_rows), block_rows)
            table_wide[at, :] = table_bf[at, :].astype(F32)
            return 0

        lax.fori_loop(0, blocks, widen, 0)
    load()

    def to_smem(place):
        return pltpu.make_async_copy(req_in.at[place], req_smem.at[place], smem_sem.at[place])

    def asked(place):
        for r in range(planes):
            request(place, r, place, r).wait()
        to_smem(place).start()

    def gather(place, r, left, right):
        def some(part, _):
            for s in range(step_rows):
                index = req_smem[place, r, 0, part * step_rows + s] & (shard_rows - 1)
                stage[s : s + 1, :] = table_wide[pl.ds(index, 1), :]
            at = pl.ds(pl.multiple_of(part * step_rows, step_rows), step_rows)
            rows = stage[...].astype(BF16)
            left[at, :] = rows[:, :half_width]
            right[at, :] = rows[:, half_width:]
            return 0

        lax.fori_loop(0, cap // step_rows, some, 0)

    foreign = pl.ds(1, planes - 1)

    def foreign_copy(side, place, slot):
        return pltpu.make_async_remote_copy(
            src_ref=rows_out.at[side, place, foreign], dst_ref=rows_in.at[side, foreign, slot],
            send_sem=rows_send.at[side, place], recv_sem=rows_recv.at[side, slot],
            device_id=across(place), device_id_type=MESH,
        )

    def near_copy(place, slot):
        return pltpu.make_async_remote_copy(
            src_ref=rows_out.at[:, place, 0], dst_ref=rows_in.at[:, 0, slot],
            send_sem=rows_send.at[2, place], recv_sem=rows_recv.at[2, slot],
            device_id=across(place), device_id_type=MESH,
        )

    def serve_foreign(step, _):
        place = around(step)

        @pl.when(step < m - 2)
        def _():
            asked(around(step + 1))

        to_smem(place).wait()
        for r in range(1, planes):
            gather(place, r, rows_out.at[0, place, r], rows_out.at[1, place, r])
        foreign_copy(0, place, q).start()
        return 0

    def serve_second(step, _):
        foreign_copy(1, around(step), q).start()
        return 0

    def collect_near(step, _):
        place = around(step)
        gather(place, 0, rows_out.at[0, place, 0], rows_out.at[1, place, 0])
        return 0

    def serve_near(step, _):
        near_copy(around(step), q).start()
        return 0

    asked(around(0))
    lax.fori_loop(0, m - 1, serve_foreign, 0)
    lax.fori_loop(0, m - 1, serve_second, 0)
    for r in range(1, planes):
        request(q, r, q, r).wait()
    to_smem(q).start()
    to_smem(q).wait()
    for r in range(planes):
        gather(q, r, rows_in.at[0, r, q], rows_in.at[1, r, q])

    code_rows[...] = jnp.zeros_like(code_rows)

    def choose(r):
        code_rows[0:bags, :] = ids[r].astype(F32)
        codes[...] = jnp.transpose(code_rows[...]).astype(jnp.int32) - plane * (m * cap)

        def some(block, _):
            place = lax.broadcasted_iota(jnp.int32, (pairs, chunk), 1) + block * chunk
            for side in range(2):
                mask = codes[:, side * half : side * half + 1] == place
                for k in range(side * half + 1, (side + 1) * half):
                    mask = mask | (codes[:, k : k + 1] == place)
                select[r, block, side * pairs : (side + 1) * pairs, :] = jnp.where(mask, 1.0, 0.0).astype(BF16)
            return 0

        lax.fori_loop(0, chunks, some, 0)

    for r in range(1, planes):
        ids_copy(r, r).wait()
        choose(r)

    def bag_sums(side, r, bag):
        rows = rows_in[side, r].reshape(m * cap, half_width)
        at = slice(bag * pairs, (bag + 1) * pairs)
        total = dot(select[r, 0, at, :], rows[:chunk])
        for block in range(1, chunks):
            total = total + dot(select[r, block, at, :], rows[block * chunk : (block + 1) * chunk])
        return total

    def part_copy(side, r, bag, slot):
        return pltpu.make_async_remote_copy(
            src_ref=part_out.at[side, r, bag], dst_ref=part_in.at[side, slot, bag],
            send_sem=part_send.at[side, r, bag], recv_sem=part_recv.at[side, slot, bag],
            device_id=column(r), device_id_type=MESH,
        )

    for side in range(2):
        def foreign_here(step, _):
            place = around(step)
            foreign_copy(side, place, place).wait()
            return 0

        if side == 1:
            lax.fori_loop(0, m - 1, collect_near, 0)
            lax.fori_loop(0, 2 * m // 3, foreign_here, 0)
            lax.fori_loop(0, m - 1, serve_near, 0)
            lax.fori_loop(2 * m // 3, m - 1, foreign_here, 0)
        else:
            lax.fori_loop(0, m - 1, foreign_here, 0)
        for bag in (1, 0):
            for r in range(1, planes):
                part_out[side, r, bag] = bag_sums(side, r, bag).astype(BF16)
                part_copy(side, r, bag, planes - r).start()

    choose(0)

    def near_here(step, _):
        place = around(step)
        near_copy(place, place).wait()
        return 0

    lax.fori_loop(0, m - 1, near_here, 0)

    def finish(bag, target):
        for side in range(2):
            total = bag_sums(side, 0, bag)
            for r in range(1, planes):
                part_copy(side, r, bag, r).wait()
                total = total + part_in[side, r, bag].astype(F32)
            target[:, side * half_width : (side + 1) * half_width] = total.astype(target.dtype)

    return finish


def lookup_scratch(grid, bags, pairs, table):
    ny, planes, cores = grid
    shard_rows, width = table.shape
    m = ny * cores
    cap = min(pairs, 3 * pairs * bags // (2 * m * planes))
    chunk = min(m * cap, 512)
    dma = pltpu.SemaphoreType.DMA
    return [
        pltpu.VMEM(table.shape, BF16),
        pltpu.VMEM(table.shape, F32),
        pltpu.VMEM((planes, bags, pairs), jnp.int32),
        pltpu.VMEM((128, pairs), F32),
        pltpu.VMEM((pairs, 128), jnp.int32),
        pltpu.VMEM((m * planes, 2 * cap), jnp.int32),
        pltpu.VMEM((m * planes, 1, 2 * cap), jnp.int32),
        pltpu.VMEM((m, planes, 1, 2 * cap), jnp.int32),
        pltpu.SMEM((m, planes, 1, 2 * cap), jnp.int32),
        pltpu.VMEM((2, m, planes, cap, width // 2), BF16),
        pltpu.VMEM((2, planes, m, cap, width // 2), BF16),
        pltpu.VMEM((planes, m * cap // chunk, 2 * pairs, chunk), BF16),
        pltpu.VMEM((32, width), F32),
        pltpu.VMEM((2, planes, 2, pairs, width // 2), BF16),
        pltpu.VMEM((2, planes, 2, pairs, width // 2), BF16),
        dma((8,)),
        dma((planes,)),
        dma((planes,)),
        dma((m, planes)),
        dma((m, planes)),
        dma((3, m)),
        dma((3, m)),
        dma((2, planes, 2)),
        dma((2, planes, 2)),
        dma((m,)),
    ]


def kernel(
    grid, nx, nz, packed_ref, table_hbm, first_hbm, second_hbm, loss_ref, item_grad_ref, query_grad_ref,
    query_ref, item_ref, first, second, slope, items, queries, exps, total_out, total_in,
    query_out, query_in, probs, item_sum, item_out, item_in, acc,
    local_sem, send_sem, recv_sem, *lookup_refs,
):
    blk = lax.axis_index("blk")
    x, z = blk // nz, blk % nz
    pairs, width = query_ref.shape
    steps, chunk = slope.shape[0], slope.shape[2]

    load_first = pltpu.make_async_copy(first_hbm, first, local_sem.at[0])
    load_second = pltpu.make_async_copy(second_hbm, second, local_sem.at[1])

    def load():
        load_first.start()
        load_second.start()

    def along_x(step):
        there = lax.rem(x + step, nx)
        return there, there * nz + z

    def along_z(step):
        there = lax.rem(z + step, nz)
        return there, x * nz + there

    def meet(barrier):
        for axis, count in ((along_x, nx), (along_z, nz)):
            for step in range(1, count):
                pl.semaphore_signal(
                    barrier, inc=1, device_id={"blk": axis(step)[1]}, device_id_type=MESH
                )
        return nx + nz - 2

    finish = lookup(grid, meet, load, packed_ref, table_hbm, lookup_refs)
    finish(1, item_ref)
    item_unit, item_scale = unit_rows(item_ref[...])
    items[z] = item_unit.astype(BF16)

    def copy(phase, source, target, landing, step, axis):
        there, device = axis(step)
        return pltpu.make_async_remote_copy(
            src_ref=source, dst_ref=target,
            send_sem=send_sem.at[phase, there], recv_sem=recv_sem.at[phase, landing],
            device_id={"blk": device}, device_id_type=MESH,
        )

    def item_copy(step, slot):
        return copy(0, items.at[z], items.at[slot], slot, step, along_z)

    def query_copy(step, slot):
        return copy(1, queries.at[x], queries.at[slot], slot, step, along_x)

    def total_copy(step, slot):
        return copy(2, total_out, total_in.at[slot], slot, step, along_x)

    def query_sum_copy(step, slot):
        there = along_x(step)[0]
        return copy(3, query_out.at[there], query_in.at[slot], slot, step, along_x)

    def item_sum_copy(step, slot):
        there = along_z(step)[0]
        return copy(4, item_out.at[there], item_in.at[slot], slot, step, along_z)

    for step in range(1, nz):
        item_copy(step, z).start()

    finish(0, query_ref)
    acc[...] = jnp.zeros_like(acc)
    load_first.wait()
    load_second.wait()

    def forward(part, _):
        at = pl.ds(pl.multiple_of(part * chunk, chunk), chunk)
        pre = dot(query_ref[...], first[:, at])
        sigma = 0.5 + 0.5 * jnp.tanh(0.5 * pre)
        slope[part] = sigma * (1.0 + pre * (1.0 - sigma))
        acc[...] += dot((pre * sigma).astype(BF16), second[at, :])
        return 0

    lax.fori_loop(0, steps, forward, 0)
    query_unit, query_scale = unit_rows(acc[...])
    queries[x] = query_unit.astype(BF16)
    for step in range(1, nx):
        query_copy(step, x).start()

    diagonal = lax.broadcasted_iota(jnp.int32, (pairs, pairs), 0) == lax.broadcasted_iota(
        jnp.int32, (pairs, pairs), 1
    )

    part = jnp.zeros((1, pairs), F32)
    own = None
    for turn in range(nz):
        zi = along_z(turn)[0]
        if turn > 0:
            item_copy(turn, zi).wait_recv()
        scores = INV_TEMP * row_dot(items[zi], queries[x])
        if turn == 0:
            own = jnp.sum(jnp.where(diagonal, scores, 0.0), axis=0, keepdims=True)
        value = jnp.exp(scores)
        exps[0, zi] = value
        part = part + jnp.sum(value, axis=0, keepdims=True)
    total_out[x] = part
    for step in range(1, nx):
        xi = along_x(step)[0]
        query_copy(step, xi).wait_recv()
        value = jnp.exp(INV_TEMP * row_dot(items[...].reshape(nz * pairs, width), queries[xi]))
        exps[step] = value.reshape(nz, pairs, pairs)
        total_out[xi] = jnp.sum(value, axis=0, keepdims=True)
    total_in[x] = total_out[...]
    for step in range(1, nx):
        total_copy(step, x).start()
    for step in range(1, nx):
        total_copy(step, along_x(step)[0]).wait_recv()

    inverse = []
    for step in range(nx):
        xi = along_x(step)[0]
        total = jnp.zeros((1, pairs), F32)
        for source in range(nx):
            total = total + total_in[source, xi]
        if step == 0:
            loss_ref[...] = jnp.log(total) - own
        inverse.append(1.0 / total)

    def item_part(zi):
        part = jnp.zeros((pairs, width), F32)
        for step in range(nx):
            prob = (exps[step, zi] * inverse[step]).astype(BF16)
            probs[step, zi] = prob
            part = part + dot(prob, queries[along_x(step)[0]])
        return part

    def query_part(step):
        return col_dot(probs[step].reshape(nz * pairs, pairs), items[...].reshape(nz * pairs, width))

    for step in range(1, nz):
        zi = along_z(step)[0]
        item_out[zi] = item_part(zi).astype(BF16)
        item_sum_copy(step, z).start()
    item_sum[...] = item_part(z)
    for step in range(1, nx):
        query_out[along_x(step)[0]] = query_part(step).astype(BF16)
        query_sum_copy(step, x).start()
    query_sum = query_part(0)

    for step in range(1, nx):
        xi = along_x(step)[0]
        query_sum_copy(step, xi).wait_recv()
        query_sum = query_sum + query_in[xi].astype(F32)
    query_unit_grad = INV_TEMP * (query_sum - items[z].astype(F32))
    query_unit = acc[...] * query_scale
    out_grad = unit_backward(query_unit_grad, query_unit, query_scale).astype(BF16)
    acc[...] = jnp.zeros_like(acc)

    def backward(part, _):
        at = pl.ds(pl.multiple_of(part * chunk, chunk), chunk)
        hidden_grad = (row_dot(out_grad, second[at, :]) * slope[part]).astype(BF16)
        acc[...] += row_dot(hidden_grad, first[:, at])
        return 0

    lax.fori_loop(0, steps, backward, 0)
    query_grad_ref[...] = acc[...]

    total_items = item_sum[...]
    for step in range(1, nz):
        zi = along_z(step)[0]
        item_sum_copy(step, zi).wait_recv()
        total_items = total_items + item_in[zi].astype(F32)
    item_unit_grad = INV_TEMP * (total_items - queries[x].astype(F32))
    item_unit, item_scale = unit_rows(item_ref[...])
    item_grad_ref[...] = unit_backward(item_unit_grad, item_unit, item_scale)

    for step in range(1, nz):
        item_copy(step, z).wait_send()
        item_sum_copy(step, z).wait_send()
    for step in range(1, nx):
        query_copy(step, x).wait_send()
        total_copy(step, x).wait_send()
        query_sum_copy(step, x).wait_send()


def local(grid, nx, nz, id_table, w_first, w_second, owner_ids, row_ids):
    pairs, bags = owner_ids.shape
    width, hidden = w_first.shape
    chunk = min(hidden, 1024)
    vmem = pl.BlockSpec(memory_space=pltpu.VMEM)
    hbm = pl.BlockSpec(memory_space=pltpu.HBM)
    most = max(nx, nz)
    loss, item_grad, query_grad = pl.pallas_call(
        functools.partial(kernel, grid, nx, nz),
        out_shape=(
            jax.ShapeDtypeStruct((1, pairs), F32),
            jax.ShapeDtypeStruct((pairs, width), F32),
            jax.ShapeDtypeStruct((pairs, width), F32),
        ),
        in_specs=[vmem, hbm, hbm, hbm],
        out_specs=(vmem, vmem, vmem),
        scratch_shapes=[
            pltpu.VMEM((pairs, width), BF16),
            pltpu.VMEM((pairs, width), F32),
            pltpu.VMEM(w_first.shape, BF16),
            pltpu.VMEM(w_second.shape, BF16),
            pltpu.VMEM((hidden // chunk, pairs, chunk), F32),
            pltpu.VMEM((nz, pairs, width), BF16),
            pltpu.VMEM((nx, pairs, width), BF16),
            pltpu.VMEM((nx, nz, pairs, pairs), F32),
            pltpu.VMEM((nx, 1, pairs), F32),
            pltpu.VMEM((nx, nx, 1, pairs), F32),
            pltpu.VMEM((nx, pairs, width), BF16),
            pltpu.VMEM((nx, pairs, width), BF16),
            pltpu.VMEM((nx, nz, pairs, pairs), BF16),
            pltpu.VMEM((pairs, width), F32),
            pltpu.VMEM((nz, pairs, width), BF16),
            pltpu.VMEM((nz, pairs, width), BF16),
            pltpu.VMEM((pairs, width), F32),
            pltpu.SemaphoreType.DMA((2,)),
            pltpu.SemaphoreType.DMA((5, most)),
            pltpu.SemaphoreType.DMA((5, most)),
            *lookup_scratch(grid, bags, pairs, id_table),
        ],
        compiler_params=pltpu.CompilerParams(
            collective_id=0, has_side_effects=True, vmem_limit_bytes=52 * 2**20
        ),
        name="step",
    )((owner_ids * id_table.shape[0] + row_ids).T, id_table, w_first, w_second)
    return loss.reshape(-1), item_grad, query_grad


def solution(mesh):
    blocks, shards = mesh.shape["blk"], mesh.shape["table"]
    nx = math.isqrt(blocks)
    nz = blocks // nx
    grid = (shards // 6, 3, 2)
    placed = (P("table", None), P(), P(), P(("blk", "table"), None), P(("blk", "table"), None))
    return jax.shard_map(
        functools.partial(local, grid, nx, nz),
        mesh=mesh,
        in_specs=placed,
        out_specs=(P(("blk", "table")), P(("blk", "table"), None), P(("blk", "table"), None)),
        check_vma=False,
    )
```
